128 devices in a mesh: energy: 8 (over z, core), views: 16 (over y, x).
Axes of the slice: x: 4, y: 4, z: 4, core: 2. Of those that a mesh axis runs over, the one named last changes fastest.
Arguments:
- projector_tiles: float32 [64, 48, 128, 256], P('views'), may hold values from -0.0546875 to 0.0546875
- tile_blocks: int32 [64, 48], P('views'), may hold values from 0 to 255
- ray_counts: int32 [64], P('views'), may hold values from 64 to 128
- sinogram: float32 [64, 8192], P('energy', 'views'), may hold values from -6 to 6
- ray_weights: float32 [64, 8192], P('energy', 'views'), may hold values from 0.25 to 4
- start_volume: float32 [64, 65536], P('energy', 'views'), may hold values from -6 to 6
- split_target: float32 [16, 64, 4096], P('views', None, 'energy'), may hold values from -6 to 6
- scaled_dual: float32 [16, 64, 4096], P('views', None, 'energy'), may hold values from -3 to 3
Outputs:
- new_volume: float32 [64, 65536], P('energy', 'views')
- new_split: float32 [16, 64, 4096], P('views', None, 'energy')
- new_dual: float32 [16, 64, 4096], P('views', None, 'energy')
The draws below stay inside these ranges and needn't reach their ends.
Inputs may be any that keep to these rules, and one draw needn't show every extreme that they name: `tile_blocks`: block indices may repeat within a ray block. `ray_counts`: rays of a block at or past its count are padding.
All inputs are finite; a program needn't handle non-finite values.
Results may differ from the reference program's by a relative error of at most 0.00022.
Values sent between devices are 32-bit elements; how exact they have to be, the bound alone decides.
A program may use at most 128 MiB of HBM per device.

```python
import math
import jax
import jax.numpy as jnp
from jax import lax

C = 64
PV = 64
RB_DEV = 4
RT = 128
VB = 256
TPR = 48
ITERS = 3
SEG = 4096
VOX = 65536
NB = 256
RAYS = 8192
N_VIEWS = 16


def place_ends(entries, key, smallest, high):
    dims = entries.shape
    place = [jax.random.randint(jax.random.fold_in(key, axis), (), 0, dims[axis]) for axis in range(len(dims))]
    entries = entries.at[tuple(place)].set(smallest)
    longest = dims.index(max(dims))
    place[longest] = (place[longest] + 1) % dims[longest]
    return entries.at[tuple(place)].set(high)


def level_of(stream_key, dims, shards, least, largest):
    def one(position, parts):
        steps = jax.random.uniform(jax.random.fold_in(jax.random.fold_in(stream_key, 6), position), (parts,), jnp.float32, least / len(shards), largest / len(shards))
        return jnp.repeat(jnp.exp(steps), dims[position] // parts).reshape((-1,) + (1,) * (len(dims) - position - 1))

    loudness = one(*shards[0])
    for cut in shards[1:]:
        loudness = loudness * one(*cut)
    return loudness


def normal_values(rng, shape, width, limit, pieces=(), kind=jnp.bfloat16):
    drawn = width * jax.random.normal(rng, shape, jnp.float32)
    if pieces:
        drawn = drawn * level_of(rng, shape, pieces, -0.22, 0.18)
    return jnp.clip(drawn, -limit, limit).astype(kind)


def setup_inputs(seed: int = 0) -> dict:
    seeds = jax.random.split(jax.random.key(seed), 9)
    return {
        "projector_tiles": normal_values(seeds[0], (N_VIEWS * RB_DEV, TPR, RT, VB), (TPR * VB) ** -0.5, 0.0546875, ((0, 16),), jnp.float32),
        "tile_blocks": place_ends(jax.random.randint(seeds[1], (N_VIEWS * RB_DEV, TPR), 0, NB), jax.random.fold_in(seeds[1], 1), 0, NB - 1).astype(jnp.int32),
        "ray_counts": place_ends(jax.random.randint(seeds[2], (N_VIEWS * RB_DEV,), RT // 2, RT + 1), jax.random.fold_in(seeds[2], 1), RT // 2, RT).astype(jnp.int32),
        "sinogram": normal_values(seeds[3], (C, RAYS), 1.0, 6.0, ((0, 8), (1, 16)), jnp.float32),
        "ray_weights": jnp.clip(jnp.exp(math.log(4.0) - 2.7725887 * jax.random.uniform(seeds[4], (C, RAYS), jnp.float32) ** level_of(seeds[4], (C, RAYS), ((0, 8), (1, 16)), -0.2, 0.2)), 0.25, 4.0),
        "start_volume": normal_values(seeds[5], (C, VOX), 1.0, 6.0, ((0, 8), (1, 16)), jnp.float32),
        "split_target": normal_values(seeds[6], (N_VIEWS, C, SEG), 1.0, 6.0, ((0, 16), (2, 8)), jnp.float32),
        "scaled_dual": normal_values(seeds[7], (N_VIEWS, C, SEG), 0.5, 3.0, ((0, 16), (2, 8)), jnp.float32),
    }


PENALTY = 1.0
SHRINK = 16.0
exact_mode = lax.Precision.HIGHEST

def forward_all(volume, projector_tiles, tile_blocks):
    channel_count = volume.shape[0]
    block_voxels = projector_tiles.shape[3]
    block_grid = volume.reshape(channel_count, -1, block_voxels)

    def one_block(pair):
        tiles_here, blocks_here = pair
        columns = block_grid[:, blocks_here]
        return jnp.einsum('ctv,tkv->ck', columns, tiles_here, precision=exact_mode)
    projected = lax.map(one_block, (projector_tiles, tile_blocks))
    return jnp.transpose(projected, (1, 0, 2)).reshape(channel_count, -1)

def backward_all(weighted, projector_tiles, tile_blocks, voxel_count):
    channel_count = weighted.shape[0]
    ray_blocks, per_block, ray_length, block_voxels = projector_tiles.shape
    ray_parts = jnp.transpose(weighted.reshape(channel_count, ray_blocks, ray_length), (1, 0, 2))

    def add_block(block_grid, triple):
        tiles_here, blocks_here, rays_here = triple
        spread_rays = jnp.einsum('ck,tkv->ctv', rays_here, tiles_here, precision=exact_mode)
        return (block_grid.at[:, blocks_here].add(spread_rays), None)
    start_grid = jnp.zeros((channel_count, voxel_count // block_voxels, block_voxels), jnp.float32)
    block_grid, unused_out = lax.scan(add_block, start_grid, (projector_tiles, tile_blocks, ray_parts))
    return block_grid.reshape(channel_count, voxel_count)

def to_volume(patched):
    return jnp.transpose(patched, (1, 0, 2)).reshape(patched.shape[1], -1)

def to_patched(volume, view_count):
    return jnp.transpose(volume.reshape(volume.shape[0], view_count, -1), (1, 0, 2))

def shrink_patches(patched):
    view_count, channel_count, segment_len = patched.shape
    blocks = patched.reshape(view_count, channel_count, segment_len // PV, PV)
    gram_matrix = jnp.einsum('acpv,adpv->apcd', blocks, blocks, precision=exact_mode)
    shifted = gram_matrix + SHRINK * jnp.eye(channel_count, dtype=jnp.float32)
    factor = jnp.linalg.cholesky(shifted)
    right_side = jnp.transpose(blocks, (0, 2, 1, 3))
    solved = jax.scipy.linalg.cho_solve((factor, True), right_side)
    shrunk = right_side - SHRINK * solved
    return jnp.transpose(shrunk, (0, 2, 1, 3)).reshape(view_count, channel_count, segment_len)

def reference(projector_tiles, tile_blocks, ray_counts, sinogram, ray_weights, start_volume, split_target, scaled_dual):
    ray_length = projector_tiles.shape[2]
    live_rays = (lax.broadcasted_iota(jnp.int32, (ray_counts.shape[0], ray_length), 1) < ray_counts[:, None]).astype(jnp.float32)
    ray_scale = ray_weights * live_rays.reshape(1, -1)
    voxel_count = start_volume.shape[1]
    target = to_volume(split_target - scaled_dual)

    def normal_map(vector, measured, anchor):
        weighted = ray_scale * (measured - forward_all(vector, projector_tiles, tile_blocks))
        return backward_all(weighted, projector_tiles, tile_blocks, voxel_count) + PENALTY * (anchor - vector)
    residual = normal_map(start_volume, sinogram, target)
    direction = residual
    volume_now = start_volume
    norm_now = jnp.sum(jnp.square(residual), axis=1)
    for iteration in range(ITERS):
        mapped = -normal_map(direction, 0.0, 0.0)
        step_size = (norm_now / jnp.sum(direction * mapped, axis=1))[:, None]
        volume_now = volume_now + step_size * direction
        residual = residual - step_size * mapped
        norm_next = jnp.sum(jnp.square(residual), axis=1)
        direction = residual + (norm_next / norm_now)[:, None] * direction
        norm_now = norm_next
    volume_patch = to_patched(volume_now, split_target.shape[0])
    new_split = shrink_patches(volume_patch + scaled_dual)
    new_dual = scaled_dual + volume_patch - new_split
    return (volume_now, new_split, new_dual)
```

```python
import functools

import jax
import jax.numpy as jnp
from jax import lax
from jax.experimental import pallas as pl
from jax.experimental.pallas import tpu as pltpu
from jax.sharding import PartitionSpec as P

PENALTY = 1.0
SHRINK = 16.0
F32 = jnp.float32
BF16 = jnp.bfloat16
NSTAGE = 4
CH = 8


def split2(v):
    hi = v.astype(BF16)
    lo = (v - hi.astype(F32)).astype(BF16)
    return hi, lo


def lane_total(v):
    return jnp.broadcast_to(jnp.sum(v, axis=1, keepdims=True), v.shape)


def main_kernel(
    idx, counts, tiles, sino, wts, x0, split, dual,
    vol_out, mb_out,
    W, stage,
    V00, V01, V10, V11, V20, V21, V30, V31,
    F, RB1, RB2, R, X, D, T, TP, MB, Pq, Q, WL, AS, AS2, AR,
    dsem, ag_s, ag_r, rs_s, rs_r, ar_s, ar_r, en_s, en_r,
):
    V = ((V00, V01), (V10, V11), (V20, V21), (V30, V31))
    e = lax.axis_index("energy")
    a = lax.axis_index("views")
    y, x = a // 4, a % 4

    def at_views(g, p, s):
        p, s = lax.rem(p + 4, 4), lax.rem(s + 4, 4)
        return {"views": s * 4 + p if g == 0 else p * 4 + s}

    coord = ((x, y), (y, x))

    barrier = pltpu.get_barrier_semaphore()
    for o in (1, 2, 3):
        pl.semaphore_signal(barrier, inc=1, device_id=at_views(0, x + o, y), device_id_type=pl.DeviceIdType.MESH)
        pl.semaphore_signal(barrier, inc=1, device_id=at_views(0, x, y + o), device_id_type=pl.DeviceIdType.MESH)
    for o in range(1, 8):
        pl.semaphore_signal(barrier, inc=1, device_id={"energy": lax.rem(e + o, 8)}, device_id_type=pl.DeviceIdType.MESH)
    pl.semaphore_wait(barrier, 13)

    def tile_copy(c, slot):
        return pltpu.make_async_copy(
            tiles.at[c // 6, pl.ds((c % 6) * CH, CH)], stage.at[slot], dsem.at[slot]
        )

    for c in range(NSTAGE):
        tile_copy(c, c).start()

    def ag(rd, h, g, k):
        p, s = coord[g]
        base = g * 128
        own = base + (s * 4 + p) * 8

        def chunk(pp):
            return base + (s * 4 + lax.rem(pp + 4, 4)) * 8

        def line(ss):
            return base + lax.rem(ss + 4, 4) * 32

        src, size, dev = {
            0: (own, 8, (p + 1, s)),
            1: (own, 8, (p - 1, s)),
            2: (chunk(p - 1), 4, (p + 1, s)),
            3: (chunk(p + 1) + 4, 4, (p - 1, s)),
            4: (line(s), 32, (p, s + 1)),
            5: (line(s), 32, (p, s - 1)),
            6: (line(s - 1), 16, (p, s + 1)),
            7: (line(s + 1) + 16, 16, (p, s - 1)),
        }[k]
        ref = V[rd][h].at[pl.ds(src, size)]
        return pltpu.make_async_remote_copy(
            src_ref=ref, dst_ref=ref,
            send_sem=ag_s.at[rd, h, g, k], recv_sem=ag_r.at[rd, h, g, k],
            device_id=at_views(g, *dev), device_id_type=pl.DeviceIdType.MESH,
        )

    def ag_step(rd, h, n):
        for g in (0, 1):
            if n > 0:
                ag(rd, h, g, 2 * n - 2).wait_recv()
                ag(rd, h, g, 2 * n - 1).wait_recv()
            if n < 4:
                ag(rd, h, g, 2 * n).start()
                ag(rd, h, g, 2 * n + 1).start()

    def ag_sent(rd):
        for h in (0, 1):
            for g in (0, 1):
                for k in range(8):
                    ag(rd, h, g, k).wait_send()

    def rs(rd, h, g, k):
        p, s = coord[g]
        base = g * 128
        kk = k % 6
        if k < 6:
            half = 16

            def row(o):
                return base + lax.rem(s + o + 4, 4) * 32

            def dev(o):
                return at_views(g, p, s + o)

            land = RB1.at[rd, h, g, kk]
        else:
            half = 4

            def row(o):
                return base + (s * 4 + lax.rem(p + o + 4, 4)) * 8

            def dev(o):
                return at_views(g, p + o, s)

            land = RB2.at[rd, h, g, kk]
        src, to = (
            (row(2), -1),
            (row(2) + half, 1),
            (row(-1) + half, -1),
            (row(1), 1),
            (row(-1), -1),
            (row(1) + half, 1),
        )[kk]
        return pltpu.make_async_remote_copy(
            src_ref=F.at[h, pl.ds(src, half)], dst_ref=land,
            send_sem=rs_s.at[rd, h, g, k], recv_sem=rs_r.at[rd, h, g, k],
            device_id=dev(to), device_id_type=pl.DeviceIdType.MESH,
        )

    def rs_step(rd, h, n):
        for g in (0, 1):
            p, s = coord[g]
            base = g * 128
            if n < 2 or n == 2:
                half, RB, k0 = 16, RB1, 0

                def row(o):
                    return base + lax.rem(s + o + 4, 4) * 32
            else:
                half, RB, k0 = 4, RB2, 6

                def row(o):
                    return base + (s * 4 + lax.rem(p + o + 4, 4)) * 8
            if n in (1, 3):
                rs(rd, h, g, k0).wait_recv()
                first = pl.ds(row(-1), half)
                F[h, first] = F[h, first] + RB[rd, h, g, 0]
                rs(rd, h, g, k0 + 4).start()
                rs(rd, h, g, k0 + 1).wait_recv()
                second = pl.ds(row(1) + half, half)
                F[h, second] = F[h, second] + RB[rd, h, g, 1]
                rs(rd, h, g, k0 + 5).start()
            if n in (2, 4):
                for k in (2, 3, 4, 5):
                    rs(rd, h, g, k0 + k).wait_recv()
                first, second = pl.ds(row(0), half), pl.ds(row(0) + half, half)
                F[h, first] = F[h, first] + RB[rd, h, g, 3] + RB[rd, h, g, 4]
                F[h, second] = F[h, second] + RB[rd, h, g, 2] + RB[rd, h, g, 5]
            if n in (0, 2):
                for k in range(4):
                    rs(rd, h, g, (0 if n == 0 else 6) + k).start()

    def rs_sent(rd):
        for h in (0, 1):
            for g in (0, 1):
                for k in range(12):
                    rs(rd, h, g, k).wait_send()

    def ar(n, k):
        src = AS if k < 3 else AS2
        o = k % 3 + 1
        dev = at_views(0, x + o, y) if k < 3 else at_views(0, x, y + o)
        return pltpu.make_async_remote_copy(
            src_ref=src.at[n], dst_ref=AR.at[n, k],
            send_sem=ar_s.at[n, k], recv_sem=ar_r.at[n, k],
            device_id=dev, device_id_type=pl.DeviceIdType.MESH,
        )

    def ar_start(n, value):
        AS[n] = value
        for k in range(3):
            ar(n, k).start()

    def ar_mid(n):
        for k in range(3):
            ar(n, k).wait_recv()
        AS2[n] = AS[n] + AR[n, 0] + AR[n, 1] + AR[n, 2]
        for k in range(3, 6):
            ar(n, k).start()

    def ar_end(n):
        for k in range(3, 6):
            ar(n, k).wait_recv()
        total = AS2[n] + AR[n, 3] + AR[n, 4] + AR[n, 5]
        for k in range(6):
            ar(n, k).wait_send()
        return lane_total(total)

    def en(n, o):
        to = lax.rem(e + o, 8)
        dst = T if n == 0 else MB
        return pltpu.make_async_remote_copy(
            src_ref=TP.at[n, to], dst_ref=dst.at[e],
            send_sem=en_s.at[n, o], recv_sem=en_r.at[n, o],
            device_id={"energy": to}, device_id_type=pl.DeviceIdType.MESH,
        )

    def own_rows(h, g):
        p, s = coord[g]
        return pl.ds(g * 128 + (s * 4 + p) * 8, 8)

    for h in (0, 1):
        for blk in range(16):
            piece = x0[:, blk * 256 + h * 128 : blk * 256 + h * 128 + 128]
            X[h, blk // 8, blk % 8] = piece
        for g in (0, 1):
            V[0][h][own_rows(h, g)] = X[h, g]
        ag_step(0, h, 0)

    for to in range(8):
        for i in (0, 1):
            for h in (0, 1):
                cols = slice(i * 256 + h * 128, i * 256 + h * 128 + 128)
                rows = slice(to * 8, to * 8 + 8)
                TP[0, to, i, h] = split[0, rows, cols] - dual[0, rows, cols]
    T[e] = TP[0, e]
    for o in range(1, 8):
        en(0, o).start()

    R[0] = jnp.zeros((8, 128), F32)

    def convert(c, carry):
        slot = lax.rem(c, NSTAGE)
        tile_copy(c, slot).wait()
        b = c // 6
        for u in range(CH // 2):
            jp = (c % 6) * (CH // 2) + u
            for h in (0, 1):
                for t in (0, 1):
                    hi, lo = split2(stage[slot, 2 * u + t, :, h * 128 : h * 128 + 128])
                    W[h, b, jp, 0:128, t * 128 : t * 128 + 128] = hi
                    W[h, b, jp, 128:256, t * 128 : t * 128 + 128] = lo

        @pl.when(c + NSTAGE < 24)
        def _():
            tile_copy(c + NSTAGE, slot).start()

        return carry

    def fwd(rd, h, lo_b, hi_b):
        def body(b, carry):
            acc = jnp.zeros((16, 256), F32)
            for jp in range(24):
                i = b * 48 + 2 * jp
                v0 = V[rd][h][idx[i]]
                v1 = V[rd][h][idx[i + 1]]
                hi, lo = split2(jnp.concatenate([v0, v1], axis=1))
                acc = acc + lax.dot_general(
                    jnp.concatenate([hi, lo], axis=0), W[h, b, jp],
                    (((1,), (1,)), ((), ())), preferred_element_type=F32,
                )
            both = acc[0:8] + acc[8:16]
            part = both[:, 0:128] + both[:, 128:256]
            if h == 0:
                Pq[b] = part
            else:
                Pq[b] = Pq[b] + part
            return carry

        lax.fori_loop(lo_b, hi_b, body, 0)

    def bwd(h, lo_b, hi_b):
        def body(b, carry):
            lhs = WL[b]
            for jp in range(24):
                i = b * 48 + 2 * jp
                out = lax.dot_general(
                    lhs, W[h, b, jp], (((1,), (0,)), ((), ())), preferred_element_type=F32
                )
                both = out[0:8] + out[8:16]
                R[i + 1] = both[:, 0:128] + R[idx[192 + i]]
                R[i + 2] = both[:, 128:256] + R[idx[193 + i]]
            return carry

        lax.fori_loop(lo_b, hi_b, body, 0)

    def scatter(h):
        def body(n, carry):
            for j in range(8):
                F[h, n * 8 + j] = R[idx[384 + n * 8 + j]]
            return carry

        lax.fori_loop(0, 32, body, 0)

    lane = lax.broadcasted_iota(jnp.int32, (8, 128), 1)

    def scale(b):
        return jnp.where(lane < counts[b], wts[:, b * 128 : b * 128 + 128], 0.0)

    def squares(v):
        return jnp.sum(v * v, axis=0)

    lax.fori_loop(0, 6, convert, 0)
    ag_step(0, 0, 1)
    ag_step(0, 1, 1)
    lax.fori_loop(6, 12, convert, 0)
    ag_step(0, 0, 2)
    ag_step(0, 1, 2)
    lax.fori_loop(12, 18, convert, 0)
    ag_step(0, 0, 3)
    lax.fori_loop(18, 24, convert, 0)
    ag_step(0, 1, 3)

    rr = None
    for rd in range(4):
        last = rd == 3
        if rd > 0:
            ag_step(rd, 0, 2)
            ag_step(rd, 1, 1)
            ag_step(rd, 0, 3)
            ag_step(rd, 1, 2)
        ag_step(rd, 0, 4)
        fwd(rd, 0, 0, 2)
        if rd > 0:
            ar_mid(2 * rd - 2)
            ag_step(rd, 1, 3)
        fwd(rd, 0, 2, 4)
        ag_step(rd, 1, 4)
        fwd(rd, 1, 0, 4)
        ag_sent(rd)
        if rd == 0:
            for b in range(4):
                w = scale(b) * (sino[:, b * 128 : b * 128 + 128] - Pq[b])
                hi, lo = split2(w)
                WL[b] = jnp.concatenate(
                    [jnp.concatenate([hi, hi], axis=1), jnp.concatenate([lo, lo], axis=1)], axis=0
                )
        else:
            rr_new = ar_end(2 * rd - 2)
            curv = jnp.zeros((8, 128), F32)
            if rd > 1:
                beta = rr_new / rr
            rr = rr_new
            for h in (0, 1):
                for g in (0, 1):
                    r_own = V[rd][h][own_rows(h, g)]
                    d_own = r_own if rd == 1 else r_own + beta * D[h, g]
                    D[h, g] = d_own
                    curv = curv + PENALTY * squares(d_own)
            for b in range(4):
                q = Pq[b] if rd == 1 else Pq[b] + beta * Q[b]
                Q[b] = q
                w = scale(b) * q
                curv = curv + w * q
                if not last:
                    hi, lo = split2(w)
                    WL[b] = jnp.concatenate(
                        [jnp.concatenate([hi, hi], axis=1), jnp.concatenate([lo, lo], axis=1)], axis=0
                    )
            ar_start(2 * rd - 1, curv)
        if not last:
            bwd(0, 0, 4)
            scatter(0)
            rs_step(rd, 0, 0)
            if rd > 0:
                ar_mid(2 * rd - 1)
            bwd(1, 0, 2)
            rs_step(rd, 0, 1)
            bwd(1, 2, 4)
            scatter(1)
            rs_step(rd, 1, 0)
            rs_step(rd, 0, 2)
            rs_step(rd, 1, 1)
            if rd > 0:
                alpha = rr / ar_end(2 * rd - 1)
            else:
                for o in range(1, 8):
                    en(0, o).wait_recv()
            rs_step(rd, 0, 3)
            rs_step(rd, 1, 2)
            norm = jnp.zeros((8, 128), F32)
            for h in (0, 1):
                rs_step(rd, h, 4)
                for g in (0, 1):
                    summed = F[h, own_rows(h, g)]
                    if rd == 0:
                        anchor = T[g * 4 : g * 4 + 4, :, h].reshape(8, 8, 128)
                        r_own = summed + PENALTY * (anchor - X[h, g])
                    else:
                        d_own = D[h, g]
                        r_own = V[rd][h][own_rows(h, g)] - alpha * (summed + PENALTY * d_own)
                        X[h, g] = X[h, g] + alpha * d_own
                    V[rd + 1][h][own_rows(h, g)] = r_own
                    norm = norm + squares(r_own)
                ag_step(rd + 1, h, 0)
                if h == 0:
                    rs_step(rd, 1, 3)
                    ag_step(rd + 1, 0, 1)
            ar_start(2 * rd, norm)
            rs_sent(rd)
        else:
            ar_mid(2 * rd - 1)
            alpha = rr / ar_end(2 * rd - 1)
            for h in (0, 1):
                for g in (0, 1):
                    X[h, g] = X[h, g] + alpha * D[h, g]
    for to in range(8):
        for i in (0, 1):
            for h in (0, 1):
                blk = 2 * to + i
                TP[1, to, i, h] = X[h, blk // 8, blk % 8]
    for o in range(1, 8):
        en(1, o).start()
    MB[e] = TP[1, e]
    for h in (0, 1):
        for blk in range(16):
            vol_out[:, blk * 256 + h * 128 : blk * 256 + h * 128 + 128] = X[h, blk // 8, blk % 8]
    for o in range(1, 8):
        en(1, o).wait_recv()
    mb_out[...] = MB[...]
    for n in (0, 1):
        for o in range(1, 8):
            en(n, o).wait_send()


def shrink_kernel(mb, dual, split_out, dual_out, M, B):
    lane = lax.broadcasted_iota(jnp.int32, (64, 128), 1)
    row = lax.broadcasted_iota(jnp.int32, (64, 128), 0)
    left = lane < 64
    for i in (0, 1):
        for h in (0, 1):
            n = i * 2 + h
            b = mb[:, i, h].reshape(64, 128) + dual[0, :, n * 128 : n * 128 + 128]
            B[n] = b
            turned = pltpu.roll(b, 64, axis=1)
            for side in (0, 1):
                one = jnp.where(left if side == 0 else lane >= 64, b, 0.0)
                gram = lax.dot_general(
                    one, jnp.concatenate([one, one], axis=0), (((1,), (1,)), ((), ())),
                    precision=lax.Precision.HIGHEST, preferred_element_type=F32,
                )
                gram = gram + jnp.where(lane == row, SHRINK, 0.0)
                M[n * 2 + side] = jnp.where(left, gram, turned if side == 0 else b)

    def step(k, carry):
        pick = jnp.full((64, 128), k, jnp.int32)
        for p in range(8):
            m = M[p]
            line = M[p, pl.ds(k, 1), :]
            col = jnp.take_along_axis(m, pick, axis=1)
            pivot = jnp.take_along_axis(jnp.broadcast_to(line, (8, 128)), pick[0:8], axis=1)[0:1]
            scaled = line / pivot
            M[p] = jnp.where(row == k, jnp.broadcast_to(scaled, (64, 128)), m - col * scaled)
        return carry

    lax.fori_loop(0, 64, step, 0)
    for i in (0, 1):
        for h in (0, 1):
            n = i * 2 + h
            solved = jnp.where(left, pltpu.roll(M[n * 2], 64, axis=1), M[n * 2 + 1])
            b = B[n]
            cols = slice(n * 128, n * 128 + 128)
            new_split = b - SHRINK * solved
            split_out[0, :, cols] = new_split
            dual_out[0, :, cols] = b - new_split


def local(tiles, tile_blocks, counts, sino, wts, x0, split, dual):
    n = tile_blocks.reshape(-1)
    tiles_here = n.shape[0]
    src, blk = n // 16, n % 16
    g = blk // 8
    place = jnp.where(g == 0, src, (src % 4) * 4 + src // 4)
    vrow = g * 128 + place * 8 + blk % 8
    order = jnp.arange(tiles_here, dtype=jnp.int32)
    same = (n[:, None] == n[None, :]) & (order[None, :] < order[:, None])
    prev = jnp.max(jnp.where(same, order[None, :] + 1, 0), axis=1)
    rows = jnp.arange(256, dtype=jnp.int32)
    final = jnp.max(jnp.where(rows[:, None] == vrow[None, :], order[None, :] + 1, 0), axis=1)
    idx = jnp.concatenate([vrow, prev, final])
    vmem = pl.BlockSpec(memory_space=pltpu.VMEM)
    smem = pl.BlockSpec(memory_space=pltpu.SMEM)
    volume, mb = pl.pallas_call(
        main_kernel,
        out_shape=(
            jax.ShapeDtypeStruct((8, 4096), F32),
            jax.ShapeDtypeStruct((8, 2, 2, 8, 128), F32),
        ),
        in_specs=[smem, smem, pl.BlockSpec(memory_space=pl.ANY)] + [vmem] * 5,
        out_specs=(vmem, vmem),
        scratch_shapes=[
            pltpu.VMEM((2, 4, 24, 256, 256), BF16),
            pltpu.VMEM((NSTAGE, CH, 128, 256), F32),
            *[pltpu.VMEM((256, 8, 128), F32)] * 8,
            pltpu.VMEM((2, 256, 8, 128), F32),
            pltpu.VMEM((3, 2, 2, 6, 16, 8, 128), F32),
            pltpu.VMEM((3, 2, 2, 6, 4, 8, 128), F32),
            pltpu.VMEM((193, 8, 128), F32),
            pltpu.VMEM((2, 2, 8, 8, 128), F32),
            pltpu.VMEM((2, 2, 8, 8, 128), F32),
            pltpu.VMEM((8, 2, 2, 8, 128), F32),
            pltpu.VMEM((2, 8, 2, 2, 8, 128), F32),
            pltpu.VMEM((8, 2, 2, 8, 128), F32),
            pltpu.VMEM((4, 8, 128), F32),
            pltpu.VMEM((4, 8, 128), F32),
            pltpu.VMEM((4, 16, 256), BF16),
            pltpu.VMEM((6, 8, 128), F32),
            pltpu.VMEM((6, 8, 128), F32),
            pltpu.VMEM((6, 6, 8, 128), F32),
            pltpu.SemaphoreType.DMA((NSTAGE,)),
            pltpu.SemaphoreType.DMA((4, 2, 2, 8)),
            pltpu.SemaphoreType.DMA((4, 2, 2, 8)),
            pltpu.SemaphoreType.DMA((3, 2, 2, 12)),
            pltpu.SemaphoreType.DMA((3, 2, 2, 12)),
            pltpu.SemaphoreType.DMA((6, 6)),
            pltpu.SemaphoreType.DMA((6, 6)),
            pltpu.SemaphoreType.DMA((2, 8)),
            pltpu.SemaphoreType.DMA((2, 8)),
        ],
        compiler_params=pltpu.CompilerParams(
            collective_id=0, has_side_effects=True, vmem_limit_bytes=56 * 1024 * 1024
        ),
        name="solve",
    )(idx, counts, tiles, sino, wts, x0, split, dual)
    new_split, new_dual = pl.pallas_call(
        shrink_kernel,
        out_shape=(jax.ShapeDtypeStruct((1, 64, 512), F32),) * 2,
        in_specs=[vmem, vmem],
        out_specs=(vmem, vmem),
        scratch_shapes=[pltpu.VMEM((8, 64, 128), F32), pltpu.VMEM((4, 64, 128), F32)],
        compiler_params=pltpu.CompilerParams(vmem_limit_bytes=16 * 1024 * 1024),
        name="shrink",
    )(mb, dual)
    return volume, new_split, new_dual


def solution(mesh):
    placed = (
        P("views", None, None, None),
        P("views", None),
        P("views"),
        P("energy", "views"),
        P("energy", "views"),
        P("energy", "views"),
        P("views", None, "energy"),
        P("views", None, "energy"),
    )
    return jax.shard_map(
        local,
        mesh=mesh,
        in_specs=placed,
        out_specs=(P("energy", "views"), P("views", None, "energy"), P("views", None, "energy")),
        check_vma=False,
    )
```

```python
import functools

import jax
import jax.numpy as jnp
from jax import lax
from jax.experimental import pallas as pl
from jax.experimental.pallas import tpu as pltpu
from jax.sharding import PartitionSpec as P

PENALTY = 1.0
SHRINK = 16.0
F32 = jnp.float32
BF16 = jnp.bfloat16
NSTAGE = 4
CH = 8


def split2(v):
    hi = v.astype(BF16)
    lo = (v - hi.astype(F32)).astype(BF16)
    return hi, lo


def lane_total(v):
    return jnp.broadcast_to(jnp.sum(v, axis=1, keepdims=True), v.shape)


def main_kernel(
    idx, counts, tiles, sino, wts, x0, split, dual,
    vol_out, mb_out,
    W, stage,
    V00, V01, V10, V11, V20, V21, V30, V31,
    F, RB1, RB2, R, X, D, T, TP, MB, Pq, Q, WL, AS, AS2, AR,
    dsem, ag_s, ag_r, rs_s, rs_r, ar_s, ar_r, en_s, en_r,
):
    V = ((V00, V01), (V10, V11), (V20, V21), (V30, V31))
    e = lax.axis_index("energy")
    a = lax.axis_index("views")
    y, x = a // 4, a % 4

    def at_views(g, p, s):
        p, s = lax.rem(p + 4, 4), lax.rem(s + 4, 4)
        return {"views": s * 4 + p if g == 0 else p * 4 + s}

    coord = ((x, y), (y, x))

    barrier = pltpu.get_barrier_semaphore()
    for o in (1, 2, 3):
        pl.semaphore_signal(barrier, inc=1, device_id=at_views(0, x + o, y), device_id_type=pl.DeviceIdType.MESH)
        pl.semaphore_signal(barrier, inc=1, device_id=at_views(0, x, y + o), device_id_type=pl.DeviceIdType.MESH)
    for o in range(1, 8):
        pl.semaphore_signal(barrier, inc=1, device_id={"energy": lax.rem(e + o, 8)}, device_id_type=pl.DeviceIdType.MESH)
    pl.semaphore_wait(barrier, 13)

    def tile_copy(c, slot):
        return pltpu.make_async_copy(
            tiles.at[c // 6, pl.ds((c % 6) * CH, CH)], stage.at[slot], dsem.at[slot]
        )

    for c in range(NSTAGE):
        tile_copy(c, c).start()

    def ag(rd, h, g, k):
        p, s = coord[g]
        base, o = g * 128, k % 3 + 1
        src, size, dst, dev = (
            (0, 8, (4 - o) * 8, (p + o, s)),
            (0, 8, (4 - o) * 32, (p, s + o)),
            (8, 24, (4 - o) * 32 + 8, (p, s + o)),
        )[k // 3]
        return pltpu.make_async_remote_copy(
            src_ref=V[rd][h].at[pl.ds(base + src, size)], dst_ref=V[rd][h].at[pl.ds(base + dst, size)],
            send_sem=ag_s.at[rd, h, g, k], recv_sem=ag_r.at[rd, h, g, k],
            device_id=at_views(g, *dev), device_id_type=pl.DeviceIdType.MESH,
        )

    def ag_step(rd, h, n):
        if n == 0:
            for k in (1, 0, 2, 4, 3, 5):
                for g in (0, 1):
                    ag(rd, h, g, k).start()
        if n == 1:
            for g in (0, 1):
                for k in (0, 1, 2):
                    ag(rd, h, g, k).wait_recv()
                for k in (7, 6, 8):
                    ag(rd, h, g, k).start()
        if n == 2:
            for g in (0, 1):
                for k in range(3, 9):
                    ag(rd, h, g, k).wait_recv()

    def ag_sent(rd):
        for h in (0, 1):
            for g in (0, 1):
                for k in range(9):
                    ag(rd, h, g, k).wait_send()

    def rs(rd, h, g, k):
        p, s = coord[g]
        base, o = g * 128, k % 3 + 1
        src, size, dev = (
            (o * 32 + 8, 24, (p, s + o)),
            (o * 32, 8, (p, s + o)),
            (o * 8, 8, (p + o, s)),
        )[k // 3]
        land = RB1.at[rd, h, g, k] if k < 3 else RB2.at[rd, h, g, k - 3]
        return pltpu.make_async_remote_copy(
            src_ref=F.at[h, pl.ds(base + src, size)], dst_ref=land,
            send_sem=rs_s.at[rd, h, g, k], recv_sem=rs_r.at[rd, h, g, k],
            device_id=at_views(g, *dev), device_id_type=pl.DeviceIdType.MESH,
        )

    def rs_step(rd, h, n):
        if n == 0:
            for k in (1, 0, 2, 4, 3, 5):
                for g in (0, 1):
                    rs(rd, h, g, k).start()
        if n == 1:
            for g in (0, 1):
                for k in (0, 1, 2):
                    rs(rd, h, g, k).wait_recv()
                line = pl.ds(g * 128 + 8, 24)
                F[h, line] = F[h, line] + RB1[rd, h, g, 0] + RB1[rd, h, g, 1] + RB1[rd, h, g, 2]
                for k in (7, 6, 8):
                    rs(rd, h, g, k).start()
        if n == 2:
            for g in (0, 1):
                for k in range(3, 9):
                    rs(rd, h, g, k).wait_recv()

    def rs_total(rd, h, g):
        total = F[h, own_rows(g)]
        for k in range(6):
            total = total + RB2[rd, h, g, k]
        return total

    def rs_sent(rd):
        for h in (0, 1):
            for g in (0, 1):
                for k in range(9):
                    rs(rd, h, g, k).wait_send()

    def ar(n, k):
        src = AS if k < 3 else AS2
        o = k % 3 + 1
        dev = at_views(0, x + o, y) if k < 3 else at_views(0, x, y + o)
        return pltpu.make_async_remote_copy(
            src_ref=src.at[n], dst_ref=AR.at[n, k],
            send_sem=ar_s.at[n, k], recv_sem=ar_r.at[n, k],
            device_id=dev, device_id_type=pl.DeviceIdType.MESH,
        )

    def ar_start(n, value):
        AS[n] = value
        for k in range(3):
            ar(n, k).start()

    def ar_mid(n):
        for k in range(3):
            ar(n, k).wait_recv()
        AS2[n] = AS[n] + AR[n, 0] + AR[n, 1] + AR[n, 2]
        for k in range(3, 6):
            ar(n, k).start()

    def ar_end(n):
        for k in range(3, 6):
            ar(n, k).wait_recv()
        total = AS2[n] + AR[n, 3] + AR[n, 4] + AR[n, 5]
        for k in range(6):
            ar(n, k).wait_send()
        return lane_total(total)

    def en(n, o):
        to = lax.rem(e + o, 8)
        dst = T if n == 0 else MB
        return pltpu.make_async_remote_copy(
            src_ref=TP.at[n, to], dst_ref=dst.at[e],
            send_sem=en_s.at[n, o], recv_sem=en_r.at[n, o],
            device_id={"energy": to}, device_id_type=pl.DeviceIdType.MESH,
        )

    def own_rows(g):
        return pl.ds(g * 128, 8)

    for h in (0, 1):
        for blk in range(16):
            piece = x0[:, blk * 256 + h * 128 : blk * 256 + h * 128 + 128]
            X[h, blk // 8, blk % 8] = piece
        for g in (0, 1):
            V[0][h][own_rows(g)] = X[h, g]
        ag_step(0, h, 0)

    for to in range(8):
        for i in (0, 1):
            for h in (0, 1):
                cols = slice(i * 256 + h * 128, i * 256 + h * 128 + 128)
                rows = slice(to * 8, to * 8 + 8)
                TP[0, to, i, h] = split[0, rows, cols] - dual[0, rows, cols]
    T[e] = TP[0, e]
    for o in range(1, 8):
        en(0, o).start()

    R[0] = jnp.zeros((8, 128), F32)

    def convert(c, carry):
        slot = lax.rem(c, NSTAGE)
        tile_copy(c, slot).wait()
        b = c // 6
        for u in range(CH // 2):
            jp = (c % 6) * (CH // 2) + u
            for h in (0, 1):
                for t in (0, 1):
                    hi, lo = split2(stage[slot, 2 * u + t, :, h * 128 : h * 128 + 128])
                    W[h, b, jp, 0:128, t * 128 : t * 128 + 128] = hi
                    W[h, b, jp, 128:256, t * 128 : t * 128 + 128] = lo

        @pl.when(c + NSTAGE < 24)
        def _():
            tile_copy(c + NSTAGE, slot).start()

        return carry

    def fwd(rd, h, lo_b, hi_b):
        def body(b, carry):
            acc = jnp.zeros((16, 256), F32)
            for jp in range(24):
                i = b * 48 + 2 * jp
                v0 = V[rd][h][idx[i]]
                v1 = V[rd][h][idx[i + 1]]
                hi, lo = split2(jnp.concatenate([v0, v1], axis=1))
                acc = acc + lax.dot_general(
                    jnp.concatenate([hi, lo], axis=0), W[h, b, jp],
                    (((1,), (1,)), ((), ())), preferred_element_type=F32,
                )
            both = acc[0:8] + acc[8:16]
            part = both[:, 0:128] + both[:, 128:256]
            if h == 0:
                Pq[b] = part
            else:
                Pq[b] = Pq[b] + part
            return carry

        lax.fori_loop(lo_b, hi_b, body, 0)

    def bwd(h, lo_b, hi_b):
        def body(b, carry):
            lhs = WL[b]
            for jp in range(24):
                i = b * 48 + 2 * jp
                out = lax.dot_general(
                    lhs, W[h, b, jp], (((1,), (0,)), ((), ())), preferred_element_type=F32
                )
                both = out[0:8] + out[8:16]
                R[i + 1] = both[:, 0:128] + R[idx[192 + i]]
                R[i + 2] = both[:, 128:256] + R[idx[193 + i]]
            return carry

        lax.fori_loop(lo_b, hi_b, body, 0)

    def scatter(h):
        def body(n, carry):
            for j in range(8):
                F[h, n * 8 + j] = R[idx[384 + n * 8 + j]]
            return carry

        lax.fori_loop(0, 32, body, 0)

    lane = lax.broadcasted_iota(jnp.int32, (8, 128), 1)

    def scale(b):
        return jnp.where(lane < counts[b], wts[:, b * 128 : b * 128 + 128], 0.0)

    def squares(v):
        return jnp.sum(v * v, axis=0)

    lax.fori_loop(0, 10, convert, 0)
    ag_step(0, 0, 1)
    ag_step(0, 1, 1)
    lax.fori_loop(10, 24, convert, 0)

    rr = None
    for rd in range(4):
        last = rd == 3
        ag_step(rd, 0, 2)
        fwd(rd, 0, 0, 2)
        if rd > 0:
            ar_mid(2 * rd - 2)
        fwd(rd, 0, 2, 4)
        ag_step(rd, 1, 2)
        fwd(rd, 1, 0, 4)
        ag_sent(rd)
        if rd == 0:
            for b in range(4):
                w = scale(b) * (sino[:, b * 128 : b * 128 + 128] - Pq[b])
                hi, lo = split2(w)
                WL[b] = jnp.concatenate(
                    [jnp.concatenate([hi, hi], axis=1), jnp.concatenate([lo, lo], axis=1)], axis=0
                )
        else:
            rr_new = ar_end(2 * rd - 2)
            curv = jnp.zeros((8, 128), F32)
            if rd > 1:
                beta = rr_new / rr
            rr = rr_new
            for h in (0, 1):
                for g in (0, 1):
                    r_own = V[rd][h][own_rows(g)]
                    d_own = r_own if rd == 1 else r_own + beta * D[h, g]
                    D[h, g] = d_own
                    curv = curv + PENALTY * squares(d_own)
            for b in range(4):
                q = Pq[b] if rd == 1 else Pq[b] + beta * Q[b]
                Q[b] = q
                w = scale(b) * q
                curv = curv + w * q
                if not last:
                    hi, lo = split2(w)
                    WL[b] = jnp.concatenate(
                        [jnp.concatenate([hi, hi], axis=1), jnp.concatenate([lo, lo], axis=1)], axis=0
                    )
            ar_start(2 * rd - 1, curv)
        if not last:
            bwd(0, 0, 4)
            scatter(0)
            rs_step(rd, 0, 0)
            bwd(1, 0, 2)
            if rd > 0:
                ar_mid(2 * rd - 1)
            bwd(1, 2, 4)
            scatter(1)
            rs_step(rd, 1, 0)
            rs_step(rd, 0, 1)
            rs_step(rd, 1, 1)
            if rd > 0:
                alpha = rr / ar_end(2 * rd - 1)
            else:
                for o in range(1, 8):
                    en(0, o).wait_recv()
            norm = jnp.zeros((8, 128), F32)
            for h in (0, 1):
                rs_step(rd, h, 2)
                for g in (0, 1):
                    summed = rs_total(rd, h, g)
                    if rd == 0:
                        anchor = T[g * 4 : g * 4 + 4, :, h].reshape(8, 8, 128)
                        r_own = summed + PENALTY * (anchor - X[h, g])
                    else:
                        d_own = D[h, g]
                        r_own = V[rd][h][own_rows(g)] - alpha * (summed + PENALTY * d_own)
                        X[h, g] = X[h, g] + alpha * d_own
                    V[rd + 1][h][own_rows(g)] = r_own
                    norm = norm + squares(r_own)
                ag_step(rd + 1, h, 0)
            ar_start(2 * rd, norm)
            ag_step(rd + 1, 0, 1)
            ag_step(rd + 1, 1, 1)
            rs_sent(rd)
        else:
            ar_mid(2 * rd - 1)
            alpha = rr / ar_end(2 * rd - 1)
            for h in (0, 1):
                for g in (0, 1):
                    X[h, g] = X[h, g] + alpha * D[h, g]
    for to in range(8):
        for i in (0, 1):
            for h in (0, 1):
                blk = 2 * to + i
                TP[1, to, i, h] = X[h, blk // 8, blk % 8]
    for o in range(1, 8):
        en(1, o).start()
    MB[e] = TP[1, e]
    for h in (0, 1):
        for blk in range(16):
            vol_out[:, blk * 256 + h * 128 : blk * 256 + h * 128 + 128] = X[h, blk // 8, blk % 8]
    for o in range(1, 8):
        en(1, o).wait_recv()
    mb_out[...] = MB[...]
    for n in (0, 1):
        for o in range(1, 8):
            en(n, o).wait_send()


def split3(v):
    a = v.astype(BF16)
    rest = v - a.astype(F32)
    b = rest.astype(BF16)
    return a, b, (rest - b.astype(F32)).astype(BF16)


def shrink_kernel(mb, dual, split_out, dual_out, M, B, GA, GB):
    lane = lax.broadcasted_iota(jnp.int32, (64, 128), 1)
    row = lax.broadcasted_iota(jnp.int32, (64, 128), 0)
    left = lane < 64
    for i in (0, 1):
        for h in (0, 1):
            n = i * 2 + h
            b = mb[:, i, h].reshape(64, 128) + dual[0, :, n * 128 : n * 128 + 128]
            B[n] = b
            turned = pltpu.roll(b, 64, axis=1)
            for side in (0, 1):
                one = jnp.where(left if side == 0 else lane >= 64, b, 0.0)
                gram = lax.dot_general(
                    one, jnp.concatenate([one, one], axis=0), (((1,), (1,)), ((), ())),
                    precision=lax.Precision.HIGHEST, preferred_element_type=F32,
                )
                gram = gram + jnp.where(lane == row, SHRINK, 0.0)
                M[n * 2 + side] = jnp.where(left, gram, turned if side == 0 else b)

    place = lax.broadcasted_iota(jnp.int32, (8, 128), 0)
    none = jnp.zeros((8, 128), F32)
    blank = jnp.zeros((16, 128), BF16)
    GA[...] = jnp.zeros_like(GA)
    GB[...] = jnp.zeros_like(GB)
    for kb in range(8):
        heads = [M[p, kb * 8 : kb * 8 + 8, :] for p in range(8)]
        for j in range(8):
            for p in range(8):
                m = heads[p]
                k = kb * 8 + j
                col = jnp.broadcast_to(m[:, k : k + 1], (8, 128))
                scaled = m[j : j + 1] / col[j : j + 1]
                heads[p] = jnp.where(place == j, scaled, m - col * scaled)
        top = slice(kb // 2 * 16, kb // 2 * 16 + 16)
        low = slice(128 + kb // 2 * 16, 144 + kb // 2 * 16)
        for p in range(8):
            if kb % 2 == 0 and kb > 0:
                for lines in (slice(kb // 2 * 16 - 16, kb // 2 * 16), slice(112 + kb // 2 * 16, 128 + kb // 2 * 16)):
                    GA[p, lines, 0:128] = blank
                    GA[p, lines, 128:256] = blank
                    GB[p, lines, :] = blank
            pair = [heads[p], none] if kb % 2 == 0 else [none, heads[p]]
            h1, h2, h3 = split3(jnp.concatenate(pair, axis=0))
            for lines in (top, low):
                GA[p, lines, 0:128] = h1
                GA[p, lines, 128:256] = h2
            GB[p, top, :] = h3
            GB[p, low, :] = h1
        for p in range(8):
            m = M[p]
            m1, m2, m3 = split3(m)
            big = jnp.dot(jnp.concatenate([m1, m2], axis=1), GA[p], preferred_element_type=F32)
            small = jnp.dot(jnp.concatenate([m1, m3], axis=1), GB[p], preferred_element_type=F32)
            M[p] = m - (big[:, 0:128] + (big[:, 128:256] + small))
            M[p, kb * 8 : kb * 8 + 8, :] = heads[p]
    for i in (0, 1):
        for h in (0, 1):
            n = i * 2 + h
            solved = jnp.where(left, pltpu.roll(M[n * 2], 64, axis=1), M[n * 2 + 1])
            b = B[n]
            cols = slice(n * 128, n * 128 + 128)
            new_split = b - SHRINK * solved
            split_out[0, :, cols] = new_split
            dual_out[0, :, cols] = b - new_split


def local(tiles, tile_blocks, counts, sino, wts, x0, split, dual):
    n = tile_blocks.reshape(-1)
    tiles_here = n.shape[0]
    src, blk = n // 16, n % 16
    g = blk // 8
    me = lax.axis_index("views")
    across, down = (src - me) % 4, (src // 4 - me // 4) % 4
    place = jnp.where(g == 0, down * 4 + across, across * 4 + down)
    vrow = g * 128 + place * 8 + blk % 8
    order = jnp.arange(tiles_here, dtype=jnp.int32)
    same = (n[:, None] == n[None, :]) & (order[None, :] < order[:, None])
    prev = jnp.max(jnp.where(same, order[None, :] + 1, 0), axis=1)
    rows = jnp.arange(256, dtype=jnp.int32)
    final = jnp.max(jnp.where(rows[:, None] == vrow[None, :], order[None, :] + 1, 0), axis=1)
    idx = jnp.concatenate([vrow, prev, final])
    vmem = pl.BlockSpec(memory_space=pltpu.VMEM)
    smem = pl.BlockSpec(memory_space=pltpu.SMEM)
    volume, mb = pl.pallas_call(
        main_kernel,
        out_shape=(
            jax.ShapeDtypeStruct((8, 4096), F32),
            jax.ShapeDtypeStruct((8, 2, 2, 8, 128), F32),
        ),
        in_specs=[smem, smem, pl.BlockSpec(memory_space=pl.ANY)] + [vmem] * 5,
        out_specs=(vmem, vmem),
        scratch_shapes=[
            pltpu.VMEM((2, 4, 24, 256, 256), BF16),
            pltpu.VMEM((NSTAGE, CH, 128, 256), F32),
            *[pltpu.VMEM((256, 8, 128), F32)] * 8,
            pltpu.VMEM((2, 256, 8, 128), F32),
            pltpu.VMEM((3, 2, 2, 3, 24, 8, 128), F32),
            pltpu.VMEM((3, 2, 2, 6, 8, 8, 128), F32),
            pltpu.VMEM((193, 8, 128), F32),
            pltpu.VMEM((2, 2, 8, 8, 128), F32),
            pltpu.VMEM((2, 2, 8, 8, 128), F32),
            pltpu.VMEM((8, 2, 2, 8, 128), F32),
            pltpu.VMEM((2, 8, 2, 2, 8, 128), F32),
            pltpu.VMEM((8, 2, 2, 8, 128), F32),
            pltpu.VMEM((4, 8, 128), F32),
            pltpu.VMEM((4, 8, 128), F32),
            pltpu.VMEM((4, 16, 256), BF16),
            pltpu.VMEM((6, 8, 128), F32),
            pltpu.VMEM((6, 8, 128), F32),
            pltpu.VMEM((6, 6, 8, 128), F32),
            pltpu.SemaphoreType.DMA((NSTAGE,)),
            pltpu.SemaphoreType.DMA((4, 2, 2, 9)),
            pltpu.SemaphoreType.DMA((4, 2, 2, 9)),
            pltpu.SemaphoreType.DMA((3, 2, 2, 9)),
            pltpu.SemaphoreType.DMA((3, 2, 2, 9)),
            pltpu.SemaphoreType.DMA((6, 6)),
            pltpu.SemaphoreType.DMA((6, 6)),
            pltpu.SemaphoreType.DMA((2, 8)),
            pltpu.SemaphoreType.DMA((2, 8)),
        ],
        compiler_params=pltpu.CompilerParams(
            collective_id=0, has_side_effects=True, vmem_limit_bytes=56 * 1024 * 1024
        ),
        name="solve",
    )(idx, counts, tiles, sino, wts, x0, split, dual)
    new_split, new_dual = pl.pallas_call(
        shrink_kernel,
        out_shape=(jax.ShapeDtypeStruct((1, 64, 512), F32),) * 2,
        in_specs=[vmem, vmem],
        out_specs=(vmem, vmem),
        scratch_shapes=[
            pltpu.VMEM((8, 64, 128), F32), pltpu.VMEM((4, 64, 128), F32),
            pltpu.VMEM((8, 256, 256), BF16), pltpu.VMEM((8, 256, 128), BF16),
        ],
        compiler_params=pltpu.CompilerParams(vmem_limit_bytes=16 * 1024 * 1024),
        name="shrink",
    )(mb, dual)
    return volume, new_split, new_dual


def solution(mesh):
    placed = (
        P("views", None, None, None),
        P("views", None),
        P("views"),
        P("energy", "views"),
        P("energy", "views"),
        P("energy", "views"),
        P("views", None, "energy"),
        P("views", None, "energy"),
    )
    return jax.shard_map(
        local,
        mesh=mesh,
        in_specs=placed,
        out_specs=(P("energy", "views"), P("views", None, "energy"), P("views", None, "energy")),
        check_vma=False,
    )
```

```python
import functools

import jax
import jax.numpy as jnp
from jax import lax
from jax.experimental import pallas as pl
from jax.experimental.pallas import tpu as pltpu
from jax.sharding import PartitionSpec as P

PENALTY = 1.0
SHRINK = 16.0
F32 = jnp.float32
BF16 = jnp.bfloat16
NSTAGE = 4
CH = 8


def split2(v):
    hi = v.astype(BF16)
    lo = (v - hi.astype(F32)).astype(BF16)
    return hi, lo


def lane_total(v):
    return jnp.broadcast_to(jnp.sum(v, axis=1, keepdims=True), v.shape)


def main_kernel(
    idx, counts, tiles, sino, wts, x0, split, dual,
    vol_out, mx_out, md_out, step_out,
    W, stage,
    V00, V01, V10, V11, V20, V21, V30, V31,
    F, RB1, RB2, R, X, D, T, TP, MX, MD, MS, SD, Pq, Q, WL, AS, AS2, AR,
    dsem, isem, ag_s, ag_r, rs_s, rs_r, ar_s, ar_r, en_s, en_r,
):
    V = ((V00, V01), (V10, V11), (V20, V21), (V30, V31))
    e = lax.axis_index("energy")
    a = lax.axis_index("views")
    y, x = a // 4, a % 4

    def at_views(g, p, s):
        p, s = lax.rem(p + 4, 4), lax.rem(s + 4, 4)
        return {"views": s * 4 + p if g == 0 else p * 4 + s}

    coord = ((x, y), (y, x))

    barrier = pltpu.get_barrier_semaphore()
    for o in (1, 2, 3):
        pl.semaphore_signal(barrier, inc=1, device_id=at_views(0, x + o, y), device_id_type=pl.DeviceIdType.MESH)
        pl.semaphore_signal(barrier, inc=1, device_id=at_views(0, x, y + o), device_id_type=pl.DeviceIdType.MESH)
    for o in range(1, 8):
        pl.semaphore_signal(barrier, inc=1, device_id={"energy": lax.rem(e + o, 8)}, device_id_type=pl.DeviceIdType.MESH)
    def tile_copy(c, slot):
        return pltpu.make_async_copy(
            tiles.at[c // 6, pl.ds((c % 6) * CH, CH)], stage.at[slot], dsem.at[slot]
        )

    def patch_copy(n):
        return pltpu.make_async_copy((split, dual)[n], SD.at[pl.ds(n, 1)], isem.at[n])

    for c in range(NSTAGE):
        tile_copy(c, c).start()
    for n in (0, 1):
        patch_copy(n).start()

    def ag(rd, h, g, k):
        p, s = coord[g]
        base, o = g * 128, k % 3 + 1
        src, size, dst, dev = (
            (0, 8, (4 - o) * 8, (p + o, s)),
            (0, 8, (4 - o) * 32, (p, s + o)),
            (8, 24, (4 - o) * 32 + 8, (p, s + o)),
        )[k // 3]
        return pltpu.make_async_remote_copy(
            src_ref=V[rd][h].at[pl.ds(base + src, size)], dst_ref=V[rd][h].at[pl.ds(base + dst, size)],
            send_sem=ag_s.at[rd, h, g, k], recv_sem=ag_r.at[rd, h, g, k],
            device_id=at_views(g, *dev), device_id_type=pl.DeviceIdType.MESH,
        )

    def ag_step(rd, h, n):
        if n == 0:
            for k in (1, 0, 2, 4, 3, 5):
                for g in (0, 1):
                    ag(rd, h, g, k).start()
        if n == 1:
            for g in (0, 1):
                for k in (0, 1, 2):
                    ag(rd, h, g, k).wait_recv()
                for k in (7, 6, 8):
                    ag(rd, h, g, k).start()
        if n == 2:
            for g in (0, 1):
                for k in range(3, 9):
                    ag(rd, h, g, k).wait_recv()

    def ag_sent(rd):
        for h in (0, 1):
            for g in (0, 1):
                for k in range(9):
                    ag(rd, h, g, k).wait_send()

    def rs(rd, h, g, k):
        p, s = coord[g]
        base, o = g * 128, k % 3 + 1
        src, size, dev = (
            (o * 32 + 8, 24, (p, s + o)),
            (o * 32, 8, (p, s + o)),
            (o * 8, 8, (p + o, s)),
        )[k // 3]
        land = RB1.at[rd, h, g, k] if k < 3 else RB2.at[rd, h, g, k - 3]
        return pltpu.make_async_remote_copy(
            src_ref=F.at[h, pl.ds(base + src, size)], dst_ref=land,
            send_sem=rs_s.at[rd, h, g, k], recv_sem=rs_r.at[rd, h, g, k],
            device_id=at_views(g, *dev), device_id_type=pl.DeviceIdType.MESH,
        )

    def rs_step(rd, h, n):
        if n == 0:
            for k in (1, 0, 2, 4, 3, 5):
                for g in (0, 1):
                    rs(rd, h, g, k).start()
        if n == 1:
            for g in (0, 1):
                for k in (0, 1, 2):
                    rs(rd, h, g, k).wait_recv()
                line = pl.ds(g * 128 + 8, 24)
                F[h, line] = F[h, line] + RB1[rd, h, g, 0] + RB1[rd, h, g, 1] + RB1[rd, h, g, 2]
                for k in (7, 6, 8):
                    rs(rd, h, g, k).start()
        if n == 2:
            for g in (0, 1):
                for k in range(3, 9):
                    rs(rd, h, g, k).wait_recv()

    def rs_total(rd, h, g):
        total = F[h, own_rows(g)]
        for k in range(6):
            total = total + RB2[rd, h, g, k]
        return total

    def rs_sent(rd):
        for h in (0, 1):
            for g in (0, 1):
                for k in range(9):
                    rs(rd, h, g, k).wait_send()

    def ar(n, k):
        src = AS if k < 3 else AS2
        o = k % 3 + 1
        dev = at_views(0, x + o, y) if k < 3 else at_views(0, x, y + o)
        return pltpu.make_async_remote_copy(
            src_ref=src.at[n], dst_ref=AR.at[n, k],
            send_sem=ar_s.at[n, k], recv_sem=ar_r.at[n, k],
            device_id=dev, device_id_type=pl.DeviceIdType.MESH,
        )

    def ar_start(n, value):
        AS[n] = value
        for k in range(3):
            ar(n, k).start()

    def ar_mid(n):
        for k in range(3):
            ar(n, k).wait_recv()
        AS2[n] = AS[n] + AR[n, 0] + AR[n, 1] + AR[n, 2]
        for k in range(3, 6):
            ar(n, k).start()

    def ar_end(n):
        for k in range(3, 6):
            ar(n, k).wait_recv()
        total = AS2[n] + AR[n, 3] + AR[n, 4] + AR[n, 5]
        for k in range(6):
            ar(n, k).wait_send()
        return lane_total(total)

    def en(n, o):
        to = lax.rem(e + o, 8)
        src = TP.at[n, to] if n < 3 else AS2.at[6]
        return pltpu.make_async_remote_copy(
            src_ref=src, dst_ref=(T, MX, MD, MS)[n].at[e],
            send_sem=en_s.at[n, o], recv_sem=en_r.at[n, o],
            device_id={"energy": to}, device_id_type=pl.DeviceIdType.MESH,
        )

    def en_volume(n, what):
        for to in range(8):
            for i in (0, 1):
                blk = 2 * to + i
                for h in (0, 1):
                    TP[n, to, i, h] = what[h, blk // 8, blk % 8]
        for o in range(1, 8):
            en(n, o).start()
        (T, MX, MD)[n][e] = TP[n, e]

    def own_rows(g):
        return pl.ds(g * 128, 8)

    for h in (0, 1):
        for blk in range(16):
            piece = x0[:, blk * 256 + h * 128 : blk * 256 + h * 128 + 128]
            X[h, blk // 8, blk % 8] = piece
        for g in (0, 1):
            V[0][h][own_rows(g)] = X[h, g]
    pl.semaphore_wait(barrier, 13)
    for h in (0, 1):
        ag_step(0, h, 0)

    for n in (0, 1):
        patch_copy(n).wait()
    for to in range(8):
        for i in (0, 1):
            for h in (0, 1):
                cols = slice(i * 256 + h * 128, i * 256 + h * 128 + 128)
                rows = slice(to * 8, to * 8 + 8)
                TP[0, to, i, h] = SD[0, rows, cols] - SD[1, rows, cols]
    T[e] = TP[0, e]
    for o in range(1, 8):
        en(0, o).start()

    R[0] = jnp.zeros((8, 128), F32)

    def convert(c, carry):
        slot = lax.rem(c, NSTAGE)
        tile_copy(c, slot).wait()
        b = c // 6
        for u in range(CH // 2):
            jp = (c % 6) * (CH // 2) + u
            for h in (0, 1):
                for t in (0, 1):
                    hi, lo = split2(stage[slot, 2 * u + t, :, h * 128 : h * 128 + 128])
                    W[h, b, jp, 0:128, t * 128 : t * 128 + 128] = hi
                    W[h, b, jp, 128:256, t * 128 : t * 128 + 128] = lo

        @pl.when(c + NSTAGE < 24)
        def _():
            tile_copy(c + NSTAGE, slot).start()

        return carry

    def fwd(rd, h, lo_b, hi_b):
        def body(b, carry):
            acc = jnp.zeros((16, 256), F32)
            for jp in range(24):
                i = b * 48 + 2 * jp
                v0 = V[rd][h][idx[i]]
                v1 = V[rd][h][idx[i + 1]]
                hi, lo = split2(jnp.concatenate([v0, v1], axis=1))
                acc = acc + lax.dot_general(
                    jnp.concatenate([hi, lo], axis=0), W[h, b, jp],
                    (((1,), (1,)), ((), ())), preferred_element_type=F32,
                )
            both = acc[0:8] + acc[8:16]
            part = both[:, 0:128] + both[:, 128:256]
            if h == 0:
                Pq[b] = part
            else:
                Pq[b] = Pq[b] + part
            return carry

        lax.fori_loop(lo_b, hi_b, body, 0)

    def bwd(h, lo_b, hi_b):
        def body(b, carry):
            lhs = WL[b]
            for jp in range(24):
                i = b * 48 + 2 * jp
                out = lax.dot_general(
                    lhs, W[h, b, jp], (((1,), (0,)), ((), ())), preferred_element_type=F32
                )
                both = out[0:8] + out[8:16]
                R[i + 1] = both[:, 0:128] + R[idx[192 + i]]
                R[i + 2] = both[:, 128:256] + R[idx[193 + i]]
            return carry

        lax.fori_loop(lo_b, hi_b, body, 0)

    def scatter(h):
        def body(n, carry):
            for j in range(8):
                F[h, n * 8 + j] = R[idx[384 + n * 8 + j]]
            return carry

        lax.fori_loop(0, 32, body, 0)

    lane = lax.broadcasted_iota(jnp.int32, (8, 128), 1)

    def scale(b):
        return jnp.where(lane < counts[b], wts[:, b * 128 : b * 128 + 128], 0.0)

    def squares(v):
        return jnp.sum(v * v, axis=0)

    lax.fori_loop(0, 10, convert, 0)
    ag_step(0, 0, 1)
    ag_step(0, 1, 1)
    lax.fori_loop(10, 24, convert, 0)

    rr = None
    for rd in range(4):
        last = rd == 3
        ag_step(rd, 0, 2)
        fwd(rd, 0, 0, 2)
        if rd > 0:
            ar_mid(2 * rd - 2)
        fwd(rd, 0, 2, 4)
        ag_step(rd, 1, 2)
        fwd(rd, 1, 0, 4)
        if rd == 0:
            for b in range(4):
                w = scale(b) * (sino[:, b * 128 : b * 128 + 128] - Pq[b])
                hi, lo = split2(w)
                WL[b] = jnp.concatenate(
                    [jnp.concatenate([hi, hi], axis=1), jnp.concatenate([lo, lo], axis=1)], axis=0
                )
        else:
            rr_new = ar_end(2 * rd - 2)
            curv = jnp.zeros((8, 128), F32)
            if rd > 1:
                beta = rr_new / rr
            rr = rr_new
            for h in (0, 1):
                for g in (0, 1):
                    r_own = V[rd][h][own_rows(g)]
                    d_own = r_own if rd == 1 else r_own + beta * D[h, g]
                    D[h, g] = d_own
                    curv = curv + PENALTY * squares(d_own)
            for b in range(4):
                q = Pq[b] if rd == 1 else Pq[b] + beta * Q[b]
                Q[b] = q
                w = scale(b) * q
                curv = curv + w * q
                if not last:
                    hi, lo = split2(w)
                    WL[b] = jnp.concatenate(
                        [jnp.concatenate([hi, hi], axis=1), jnp.concatenate([lo, lo], axis=1)], axis=0
                    )
            ar_start(2 * rd - 1, curv)
        if not last:
            bwd(0, 0, 4)
            scatter(0)
            rs_step(rd, 0, 0)
            bwd(1, 0, 2)
            if rd > 0:
                ar_mid(2 * rd - 1)
            bwd(1, 2, 4)
            scatter(1)
            rs_step(rd, 1, 0)
            ag_sent(rd)
            rs_step(rd, 0, 1)
            rs_step(rd, 1, 1)
            if rd > 0:
                alpha = rr / ar_end(2 * rd - 1)
            else:
                for o in range(1, 8):
                    en(0, o).wait_recv()
            norm = jnp.zeros((8, 128), F32)
            for h in (0, 1):
                rs_step(rd, h, 2)
                for g in (0, 1):
                    summed = rs_total(rd, h, g)
                    if rd == 0:
                        anchor = T[g * 4 : g * 4 + 4, :, h].reshape(8, 8, 128)
                        r_own = summed + PENALTY * (anchor - X[h, g])
                    else:
                        d_own = D[h, g]
                        r_own = V[rd][h][own_rows(g)] - alpha * (summed + PENALTY * d_own)
                        X[h, g] = X[h, g] + alpha * d_own
                    V[rd + 1][h][own_rows(g)] = r_own
                    norm = norm + squares(r_own)
                ag_step(rd + 1, h, 0)
            ar_start(2 * rd, norm)
            ag_step(rd + 1, 0, 1)
            ag_step(rd + 1, 1, 1)
            rs_sent(rd)
            if rd == 2:
                en_volume(1, X)
        else:
            en_volume(2, D)
            ag_sent(rd)
            ar_mid(2 * rd - 1)
            alpha = rr / ar_end(2 * rd - 1)
            AS2[6] = alpha
            MS[e] = alpha
            for o in range(1, 8):
                en(3, o).start()
            for h in (0, 1):
                for blk in range(16):
                    cols = slice(blk * 256 + h * 128, blk * 256 + h * 128 + 128)
                    vol_out[:, cols] = X[h, blk // 8, blk % 8] + alpha * D[h, blk // 8, blk % 8]
    for n in (1, 2, 3):
        for o in range(1, 8):
            en(n, o).wait_recv()
        (mx_out, md_out, step_out)[n - 1][...] = (MX, MD, MS)[n - 1][...]
    for n in range(4):
        for o in range(1, 8):
            en(n, o).wait_send()


def split3(v):
    a = v.astype(BF16)
    rest = v - a.astype(F32)
    b = rest.astype(BF16)
    return a, b, (rest - b.astype(F32)).astype(BF16)


def shrink_kernel(mx, md, step, dual, vol, vol_out, split_out, dual_out, M, B, GA, GB):
    vol_out[...] = vol[...]
    steps = step[...].reshape(64, 128)
    lane = lax.broadcasted_iota(jnp.int32, (64, 128), 1)
    row = lax.broadcasted_iota(jnp.int32, (64, 128), 0)
    left = lane < 64
    for i in (0, 1):
        for h in (0, 1):
            n = i * 2 + h
            volume = mx[:, i, h].reshape(64, 128) + steps * md[:, i, h].reshape(64, 128)
            b = volume + dual[0, :, n * 128 : n * 128 + 128]
            B[n] = b
            turned = pltpu.roll(b, 64, axis=1)
            for side in (0, 1):
                one = jnp.where(left if side == 0 else lane >= 64, b, 0.0)
                gram = lax.dot_general(
                    one, jnp.concatenate([one, one], axis=0), (((1,), (1,)), ((), ())),
                    precision=lax.Precision.HIGHEST, preferred_element_type=F32,
                )
                gram = gram + jnp.where(lane == row, SHRINK, 0.0)
                M[n * 2 + side] = jnp.where(left, gram, turned if side == 0 else b)

    place = lax.broadcasted_iota(jnp.int32, (8, 128), 0)
    none = jnp.zeros((8, 128), F32)
    blank = jnp.zeros((16, 128), BF16)
    GA[...] = jnp.zeros_like(GA)
    GB[...] = jnp.zeros_like(GB)
    for kb in range(8):
        heads = [M[p, kb * 8 : kb * 8 + 8, :] for p in range(8)]
        for j in range(8):
            for p in range(8):
                m = heads[p]
                k = kb * 8 + j
                col = jnp.broadcast_to(m[:, k : k + 1], (8, 128))
                scaled = m[j : j + 1] / col[j : j + 1]
                heads[p] = jnp.where(place == j, scaled, m - col * scaled)
        top = slice(kb // 2 * 16, kb // 2 * 16 + 16)
        low = slice(128 + kb // 2 * 16, 144 + kb // 2 * 16)
        for p in range(8):
            if kb % 2 == 0 and kb > 0:
                for lines in (slice(kb // 2 * 16 - 16, kb // 2 * 16), slice(112 + kb // 2 * 16, 128 + kb // 2 * 16)):
                    GA[p, lines, 0:128] = blank
                    GA[p, lines, 128:256] = blank
                    GB[p, lines, :] = blank
            pair = [heads[p], none] if kb % 2 == 0 else [none, heads[p]]
            h1, h2, h3 = split3(jnp.concatenate(pair, axis=0))
            for lines in (top, low):
                GA[p, lines, 0:128] = h1
                GA[p, lines, 128:256] = h2
            GB[p, top, :] = h3
            GB[p, low, :] = h1
        for p in range(8):
            m = M[p]
            m1, m2, m3 = split3(m)
            big = jnp.dot(jnp.concatenate([m1, m2], axis=1), GA[p], preferred_element_type=F32)
            small = jnp.dot(jnp.concatenate([m1, m3], axis=1), GB[p], preferred_element_type=F32)
            M[p] = m - (big[:, 0:128] + (big[:, 128:256] + small))
            M[p, kb * 8 : kb * 8 + 8, :] = heads[p]
    for i in (0, 1):
        for h in (0, 1):
            n = i * 2 + h
            solved = jnp.where(left, pltpu.roll(M[n * 2], 64, axis=1), M[n * 2 + 1])
            b = B[n]
            cols = slice(n * 128, n * 128 + 128)
            new_split = b - SHRINK * solved
            split_out[0, :, cols] = new_split
            dual_out[0, :, cols] = b - new_split


def local(tiles, tile_blocks, counts, sino, wts, x0, split, dual):
    n = tile_blocks.reshape(-1)
    tiles_here = n.shape[0]
    src, blk = n // 16, n % 16
    g = blk // 8
    me = lax.axis_index("views")
    across, down = (src - me) % 4, (src // 4 - me // 4) % 4
    place = jnp.where(g == 0, down * 4 + across, across * 4 + down)
    vrow = g * 128 + place * 8 + blk % 8
    order = jnp.arange(tiles_here, dtype=jnp.int32)
    same = (n[:, None] == n[None, :]) & (order[None, :] < order[:, None])
    prev = jnp.max(jnp.where(same, order[None, :] + 1, 0), axis=1)
    rows = jnp.arange(256, dtype=jnp.int32)
    final = jnp.max(jnp.where(rows[:, None] == vrow[None, :], order[None, :] + 1, 0), axis=1)
    idx = jnp.concatenate([vrow, prev, final])
    vmem = pl.BlockSpec(memory_space=pltpu.VMEM)
    smem = pl.BlockSpec(memory_space=pltpu.SMEM)
    anywhere = pl.BlockSpec(memory_space=pl.ANY)
    volume, mx, md, step = pl.pallas_call(
        main_kernel,
        out_shape=(
            jax.ShapeDtypeStruct((8, 4096), F32),
            jax.ShapeDtypeStruct((8, 2, 2, 8, 128), F32),
            jax.ShapeDtypeStruct((8, 2, 2, 8, 128), F32),
            jax.ShapeDtypeStruct((8, 8, 128), F32),
        ),
        in_specs=[smem, smem, anywhere, vmem, vmem, vmem, anywhere, anywhere],
        out_specs=(vmem,) * 4,
        scratch_shapes=[
            pltpu.VMEM((2, 4, 24, 256, 256), BF16),
            pltpu.VMEM((NSTAGE, CH, 128, 256), F32),
            *[pltpu.VMEM((256, 8, 128), F32)] * 8,
            pltpu.VMEM((2, 256, 8, 128), F32),
            pltpu.VMEM((3, 2, 2, 3, 24, 8, 128), F32),
            pltpu.VMEM((3, 2, 2, 6, 8, 8, 128), F32),
            pltpu.VMEM((193, 8, 128), F32),
            pltpu.VMEM((2, 2, 8, 8, 128), F32),
            pltpu.VMEM((2, 2, 8, 8, 128), F32),
            pltpu.VMEM((8, 2, 2, 8, 128), F32),
            pltpu.VMEM((3, 8, 2, 2, 8, 128), F32),
            pltpu.VMEM((8, 2, 2, 8, 128), F32),
            pltpu.VMEM((8, 2, 2, 8, 128), F32),
            pltpu.VMEM((8, 8, 128), F32),
            pltpu.VMEM((2, 64, 512), F32),
            pltpu.VMEM((4, 8, 128), F32),
            pltpu.VMEM((4, 8, 128), F32),
            pltpu.VMEM((4, 16, 256), BF16),
            pltpu.VMEM((6, 8, 128), F32),
            pltpu.VMEM((7, 8, 128), F32),
            pltpu.VMEM((6, 6, 8, 128), F32),
            pltpu.SemaphoreType.DMA((NSTAGE,)),
            pltpu.SemaphoreType.DMA((2,)),
            pltpu.SemaphoreType.DMA((4, 2, 2, 9)),
            pltpu.SemaphoreType.DMA((4, 2, 2, 9)),
            pltpu.SemaphoreType.DMA((3, 2, 2, 9)),
            pltpu.SemaphoreType.DMA((3, 2, 2, 9)),
            pltpu.SemaphoreType.DMA((6, 6)),
            pltpu.SemaphoreType.DMA((6, 6)),
            pltpu.SemaphoreType.DMA((4, 8)),
            pltpu.SemaphoreType.DMA((4, 8)),
        ],
        compiler_params=pltpu.CompilerParams(
            collective_id=0, has_side_effects=True, vmem_limit_bytes=56 * 1024 * 1024
        ),
        name="solve",
    )(idx, counts, tiles, sino, wts, x0, split, dual)
    volume, new_split, new_dual = pl.pallas_call(
        shrink_kernel,
        out_shape=(jax.ShapeDtypeStruct((8, 4096), F32),) + (jax.ShapeDtypeStruct((1, 64, 512), F32),) * 2,
        in_specs=[vmem] * 5,
        out_specs=(vmem,) * 3,
        scratch_shapes=[
            pltpu.VMEM((8, 64, 128), F32), pltpu.VMEM((4, 64, 128), F32),
            pltpu.VMEM((8, 256, 256), BF16), pltpu.VMEM((8, 256, 128), BF16),
        ],
        compiler_params=pltpu.CompilerParams(vmem_limit_bytes=16 * 1024 * 1024),
        name="shrink",
    )(mx, md, step, dual, volume)
    return volume, new_split, new_dual


def solution(mesh):
    placed = (
        P("views", None, None, None),
        P("views", None),
        P("views"),
        P("energy", "views"),
        P("energy", "views"),
        P("energy", "views"),
        P("views", None, "energy"),
        P("views", None, "energy"),
    )
    return jax.shard_map(
        local,
        mesh=mesh,
        in_specs=placed,
        out_specs=(P("energy", "views"), P("views", None, "energy"), P("views", None, "energy")),
        check_vma=False,
    )
```

```python
import functools

import jax
import jax.numpy as jnp
from jax import lax
from jax.experimental import pallas as pl
from jax.experimental.pallas import tpu as pltpu
from jax.sharding import PartitionSpec as P

PENALTY = 1.0
SHRINK = 16.0
F32 = jnp.float32
BF16 = jnp.bfloat16
NSTAGE = 4
CH = 8


def split2(v):
    hi = v.astype(BF16)
    lo = (v - hi.astype(F32)).astype(BF16)
    return hi, lo


def lane_total(v):
    return jnp.broadcast_to(jnp.sum(v, axis=1, keepdims=True), v.shape)


def main_kernel(
    idx, counts, tiles, sino, wts, x0, split, dual,
    vol_out, mx_out, md_out, step_out,
    W, stage,
    V00, V01, V10, V11, V20, V21, V30, V31,
    F, RB1, RB2, R, X, D, T, TP, MX, MD, MS, SD, XS, RS, VO, Pq, Q, WL, AS, AS2, AR,
    dsem, isem, osem, ag_s, ag_r, rs_s, rs_r, ar_s, ar_r, en_s, en_r,
):
    V = ((V00, V01), (V10, V11), (V20, V21), (V30, V31))
    e = lax.axis_index("energy")
    a = lax.axis_index("views")
    y, x = a // 4, a % 4

    def at_views(g, p, s):
        p, s = lax.rem(p + 4, 4), lax.rem(s + 4, 4)
        return {"views": s * 4 + p if g == 0 else p * 4 + s}

    coord = ((x, y), (y, x))

    barrier = pltpu.get_barrier_semaphore()
    for o in (1, 2, 3):
        pl.semaphore_signal(barrier, inc=1, device_id=at_views(0, x + o, y), device_id_type=pl.DeviceIdType.MESH)
        pl.semaphore_signal(barrier, inc=1, device_id=at_views(0, x, y + o), device_id_type=pl.DeviceIdType.MESH)
    for o in range(1, 8):
        pl.semaphore_signal(barrier, inc=1, device_id={"energy": lax.rem(e + o, 8)}, device_id_type=pl.DeviceIdType.MESH)

    def tile_copy(c, slot):
        return pltpu.make_async_copy(
            tiles.at[c // 6, pl.ds((c % 6) * CH, CH)], stage.at[slot], dsem.at[slot]
        )

    def read(n):
        to = (SD.at[pl.ds(0, 1)], SD.at[pl.ds(1, 1)], XS, RS.at[0], RS.at[1])[n]
        return pltpu.make_async_copy((split, dual, x0, sino, wts)[n], to, isem.at[n])

    def write(n):
        return pltpu.make_async_copy((MX, MD, MS, VO)[n], (mx_out, md_out, step_out, vol_out)[n], osem.at[n])


    for n in (2, 0, 1, 3, 4):
        read(n).start()
    for c in range(NSTAGE):
        tile_copy(c, c).start()

    def ag(rd, h, g, k):
        p, s = coord[g]
        base, o = g * 128, k % 3 + 1
        src, size, dst, dev = (
            (0, 8, (4 - o) * 8, (p + o, s)),
            (0, 8, (4 - o) * 32, (p, s + o)),
            (8, 24, (4 - o) * 32 + 8, (p, s + o)),
        )[k // 3]
        return pltpu.make_async_remote_copy(
            src_ref=V[rd][h].at[pl.ds(base + src, size)], dst_ref=V[rd][h].at[pl.ds(base + dst, size)],
            send_sem=ag_s.at[rd, h, g], recv_sem=ag_r.at[rd, h, g, min(k // 3, 1)],
            device_id=at_views(g, *dev), device_id_type=pl.DeviceIdType.MESH,
        )

    def ag_bytes(rd, h, g, size, k):
        return pltpu.make_async_remote_copy(
            src_ref=V[rd][h].at[pl.ds(0, size)], dst_ref=V[rd][h].at[pl.ds(0, size)],
            send_sem=ag_s.at[rd, h, g], recv_sem=ag_r.at[rd, h, g, k],
            device_id=at_views(g, coord[g][0] + 1, coord[g][1]), device_id_type=pl.DeviceIdType.MESH,
        )

    def ag_step(rd, h, n):
        if n == 0:
            for k in (1, 0, 2, 4, 3, 5):
                for g in (0, 1):
                    ag(rd, h, g, k).start()
        if n == 1:
            for g in (0, 1):
                ag_bytes(rd, h, g, 24, 0).wait_recv()
                for k in (7, 6, 8):
                    ag(rd, h, g, k).start()
        if n == 2:
            for g in (0, 1):
                ag_bytes(rd, h, g, 96, 1).wait_recv()

    def ag_sent(rd):
        for h in (0, 1):
            for g in (0, 1):
                ag_bytes(rd, h, g, 120, 0).wait_send()

    def rs(rd, h, g, k):
        p, s = coord[g]
        base, o = g * 128, k % 3 + 1
        src, size, dev = (
            (o * 32 + 8, 24, (p, s + o)),
            (o * 32, 8, (p, s + o)),
            (o * 8, 8, (p + o, s)),
        )[k // 3]
        land = RB1.at[rd, h, g, k] if k < 3 else RB2.at[rd, h, g, k - 3]
        return pltpu.make_async_remote_copy(
            src_ref=F.at[h, pl.ds(base + src, size)], dst_ref=land,
            send_sem=rs_s.at[rd, h, g], recv_sem=rs_r.at[rd, h, g, min(k // 3, 1)],
            device_id=at_views(g, *dev), device_id_type=pl.DeviceIdType.MESH,
        )

    def rs_bytes(rd, h, g, size, k):
        return pltpu.make_async_remote_copy(
            src_ref=F.at[h, pl.ds(0, size)], dst_ref=F.at[h, pl.ds(0, size)],
            send_sem=rs_s.at[rd, h, g], recv_sem=rs_r.at[rd, h, g, k],
            device_id=at_views(g, coord[g][0] + 1, coord[g][1]), device_id_type=pl.DeviceIdType.MESH,
        )

    def rs_step(rd, h, n):
        if n == 0:
            for k in (1, 0, 2, 4, 3, 5):
                for g in (0, 1):
                    rs(rd, h, g, k).start()
        if n == 1:
            for g in (0, 1):
                rs_bytes(rd, h, g, 72, 0).wait_recv()
                line = pl.ds(g * 128 + 8, 24)
                F[h, line] = F[h, line] + RB1[rd, h, g, 0] + RB1[rd, h, g, 1] + RB1[rd, h, g, 2]
                for k in (7, 6, 8):
                    rs(rd, h, g, k).start()
        if n == 2:
            for g in (0, 1):
                rs_bytes(rd, h, g, 48, 1).wait_recv()

    def rs_total(rd, h, g):
        total = F[h, own_rows(g)]
        for k in range(6):
            total = total + RB2[rd, h, g, k]
        return total

    def rs_sent(rd):
        for h in (0, 1):
            for g in (0, 1):
                rs_bytes(rd, h, g, 120, 0).wait_send()

    def ar(n, k):
        src = AS if k < 3 else AS2
        o = k % 3 + 1
        dev = at_views(0, x + o, y) if k < 3 else at_views(0, x, y + o)
        return pltpu.make_async_remote_copy(
            src_ref=src.at[n], dst_ref=AR.at[n, k],
            send_sem=ar_s.at[n, k], recv_sem=ar_r.at[n, k],
            device_id=dev, device_id_type=pl.DeviceIdType.MESH,
        )

    def ar_start(n, value):
        AS[n] = value
        for k in range(3):
            ar(n, k).start()

    def ar_mid(n):
        for k in range(3):
            ar(n, k).wait_recv()
        AS2[n] = AS[n] + AR[n, 0] + AR[n, 1] + AR[n, 2]
        for k in range(3, 6):
            ar(n, k).start()

    def ar_end(n):
        for k in range(3, 6):
            ar(n, k).wait_recv()
        total = AS2[n] + AR[n, 3] + AR[n, 4] + AR[n, 5]
        for k in range(6):
            ar(n, k).wait_send()
        return lane_total(total)

    def en(n, o):
        to = lax.rem(e + o, 8)
        src = TP.at[n, to] if n < 3 else AS2.at[6]
        return pltpu.make_async_remote_copy(
            src_ref=src, dst_ref=(T, MX, MD, MS)[n].at[e],
            send_sem=en_s.at[n, o], recv_sem=en_r.at[n, o],
            device_id={"energy": to}, device_id_type=pl.DeviceIdType.MESH,
        )

    def en_volume(n, what):
        for to in range(8):
            for i in (0, 1):
                blk = 2 * to + i
                for h in (0, 1):
                    TP[n, to, i, h] = what[h, blk // 8, blk % 8]
        for o in range(1, 8):
            en(n, o).start()
        (T, MX, MD)[n][e] = TP[n, e]

    def own_rows(g):
        return pl.ds(g * 128, 8)

    read(2).wait()
    for h in (0, 1):
        for blk in range(16):
            piece = XS[:, blk * 256 + h * 128 : blk * 256 + h * 128 + 128]
            X[h, blk // 8, blk % 8] = piece
        for g in (0, 1):
            V[0][h][own_rows(g)] = X[h, g]
    pl.semaphore_wait(barrier, 13)
    for h in (0, 1):
        ag_step(0, h, 0)

    for n in (0, 1, 3, 4):
        read(n).wait()
    for to in range(8):
        for i in (0, 1):
            for h in (0, 1):
                cols = slice(i * 256 + h * 128, i * 256 + h * 128 + 128)
                rows = slice(to * 8, to * 8 + 8)
                TP[0, to, i, h] = SD[0, rows, cols] - SD[1, rows, cols]
    T[e] = TP[0, e]
    for o in range(1, 8):
        en(0, o).start()

    R[0] = jnp.zeros((8, 128), F32)

    def convert(c, carry):
        slot = lax.rem(c, NSTAGE)
        tile_copy(c, slot).wait()
        b = c // 6
        for u in range(CH // 2):
            jp = (c % 6) * (CH // 2) + u
            for h in (0, 1):
                for t in (0, 1):
                    part = stage[slot, 2 * u + t, :, h * 128 : h * 128 + 128]
                    here = slice(t * 128, t * 128 + 128)
                    if h == 0:
                        W[h, b, jp, 0:128, here], W[h, b, jp, 128:256, here] = split2(part)
                    else:
                        W[h, b, jp, here, 0:128], W[h, b, jp, here, 128:256] = split2(part.T)

        @pl.when(c + NSTAGE < 24)
        def _():
            tile_copy(c + NSTAGE, slot).start()

        return carry

    def fwd(rd, h, lo_b, hi_b):
        def body(b, carry):
            acc = jnp.zeros((16, 256), F32)
            for jp in range(24):
                i = b * 48 + 2 * jp
                v0 = V[rd][h][idx[i]]
                v1 = V[rd][h][idx[i + 1]]
                hi, lo = split2(jnp.concatenate([v0, v1], axis=1))
                acc = acc + lax.dot_general(
                    jnp.concatenate([hi, lo], axis=0), W[h, b, jp],
                    (((1,), (1 - h,)), ((), ())), preferred_element_type=F32,
                )
            both = acc[0:8] + acc[8:16]
            part = both[:, 0:128] + both[:, 128:256]
            if h == 0:
                Pq[b] = part
            else:
                Pq[b] = Pq[b] + part
            return carry

        lax.fori_loop(lo_b, hi_b, body, 0)

    def bwd(h, lo_b, hi_b):
        def body(b, carry):
            lhs = WL[b]
            for jp in range(24):
                i = b * 48 + 2 * jp
                out = lax.dot_general(
                    lhs, W[h, b, jp], (((1,), (h,)), ((), ())), preferred_element_type=F32
                )
                both = out[0:8] + out[8:16]
                R[i + 1] = both[:, 0:128] + R[idx[192 + i]]
                R[i + 2] = both[:, 128:256] + R[idx[193 + i]]
            return carry

        lax.fori_loop(lo_b, hi_b, body, 0)

    def scatter(h):
        def body(n, carry):
            for j in range(8):
                F[h, n * 8 + j] = R[idx[384 + n * 8 + j]]
            return carry

        lax.fori_loop(0, 32, body, 0)

    lane = lax.broadcasted_iota(jnp.int32, (8, 128), 1)

    def scale(b):
        return jnp.where(lane < counts[b], RS[1, :, b * 128 : b * 128 + 128], 0.0)

    def squares(v):
        return jnp.sum(v * v, axis=0)

    lax.fori_loop(0, 10, convert, 0)
    ag_step(0, 0, 1)
    ag_step(0, 1, 1)
    lax.fori_loop(10, 24, convert, 0)

    rr = None
    for rd in range(4):
        last = rd == 3
        ag_step(rd, 0, 2)
        fwd(rd, 0, 0, 2)
        if rd > 0:
            ar_mid(2 * rd - 2)
        fwd(rd, 0, 2, 4)
        ag_step(rd, 1, 2)
        fwd(rd, 1, 0, 4)
        if rd == 0:
            for b in range(4):
                w = scale(b) * (RS[0, :, b * 128 : b * 128 + 128] - Pq[b])
                hi, lo = split2(w)
                WL[b] = jnp.concatenate(
                    [jnp.concatenate([hi, hi], axis=1), jnp.concatenate([lo, lo], axis=1)], axis=0
                )
        else:
            rr_new = ar_end(2 * rd - 2)
            curv = jnp.zeros((8, 128), F32)
            if rd > 1:
                beta = rr_new / rr
            rr = rr_new
            for h in (0, 1):
                for g in (0, 1):
                    r_own = V[rd][h][own_rows(g)]
                    d_own = r_own if rd == 1 else r_own + beta * D[h, g]
                    D[h, g] = d_own
                    curv = curv + PENALTY * squares(d_own)
            for b in range(4):
                q = Pq[b] if rd == 1 else Pq[b] + beta * Q[b]
                Q[b] = q
                w = scale(b) * q
                curv = curv + w * q
                if not last:
                    hi, lo = split2(w)
                    WL[b] = jnp.concatenate(
                        [jnp.concatenate([hi, hi], axis=1), jnp.concatenate([lo, lo], axis=1)], axis=0
                    )
            ar_start(2 * rd - 1, curv)
        if not last:
            bwd(0, 0, 4)
            scatter(0)
            rs_step(rd, 0, 0)
            bwd(1, 0, 2)
            if rd > 0:
                ar_mid(2 * rd - 1)
            bwd(1, 2, 4)
            scatter(1)
            rs_step(rd, 1, 0)
            ag_sent(rd)
            rs_step(rd, 0, 1)
            rs_step(rd, 1, 1)
            if rd > 0:
                alpha = rr / ar_end(2 * rd - 1)
            else:
                for o in range(1, 8):
                    en(0, o).wait_recv()
            norm = jnp.zeros((8, 128), F32)
            for h in (0, 1):
                rs_step(rd, h, 2)
                for g in (0, 1):
                    summed = rs_total(rd, h, g)
                    if rd == 0:
                        anchor = T[g * 4 : g * 4 + 4, :, h].reshape(8, 8, 128)
                        r_own = summed + PENALTY * (anchor - X[h, g])
                    else:
                        d_own = D[h, g]
                        r_own = V[rd][h][own_rows(g)] - alpha * (summed + PENALTY * d_own)
                        X[h, g] = X[h, g] + alpha * d_own
                    V[rd + 1][h][own_rows(g)] = r_own
                    norm = norm + squares(r_own)
                ag_step(rd + 1, h, 0)
            ar_start(2 * rd, norm)
            ag_step(rd + 1, 0, 1)
            ag_step(rd + 1, 1, 1)
            rs_sent(rd)
            if rd == 2:
                en_volume(1, X)
        else:
            en_volume(2, D)
            ag_sent(rd)
            ar_mid(2 * rd - 1)
            alpha = rr / ar_end(2 * rd - 1)
            AS2[6] = alpha
            MS[e] = alpha
            for o in range(1, 8):
                en(3, o).start()
            for h in (0, 1):
                for blk in range(16):
                    cols = slice(blk * 256 + h * 128, blk * 256 + h * 128 + 128)
                    VO[:, cols] = X[h, blk // 8, blk % 8] + alpha * D[h, blk // 8, blk % 8]
    write(3).start()
    for n in (1, 2, 3):
        for o in range(1, 8):
            en(n, o).wait_recv()
        write(n - 1).start()
    for n in range(4):
        for o in range(1, 8):
            en(n, o).wait_send()
    for n in range(4):
        write(n).wait()


def split3(v):
    a = v.astype(BF16)
    rest = v - a.astype(F32)
    b = rest.astype(BF16)
    return a, b, (rest - b.astype(F32)).astype(BF16)


def shrink_kernel(
    mx_in, md_in, step_in, dual_in, vol, vol_out, split_out, dual_out,
    mx, md, step, dual, SO, DO, M, B, GA, GB, isem, osem,
):
    passed = pltpu.make_async_copy(vol, vol_out, isem.at[4])
    passed.start()
    reads = [
        pltpu.make_async_copy(a, b, isem.at[n])
        for n, (a, b) in enumerate(((mx_in, mx), (md_in, md), (step_in, step), (dual_in, dual)))
    ]
    for one in reads:
        one.start()
    GA[...] = jnp.zeros_like(GA)
    GB[...] = jnp.zeros_like(GB)
    for one in reads:
        one.wait()
    steps = step[...].reshape(64, 128)
    lane = lax.broadcasted_iota(jnp.int32, (64, 128), 1)
    row = lax.broadcasted_iota(jnp.int32, (64, 128), 0)
    left = lane < 64
    for i in (0, 1):
        for h in (0, 1):
            n = i * 2 + h
            volume = mx[:, i, h].reshape(64, 128) + steps * md[:, i, h].reshape(64, 128)
            b = volume + dual[0, :, n * 128 : n * 128 + 128]
            B[n] = b
            turned = pltpu.roll(b, 64, axis=1)
            for side in (0, 1):
                one = jnp.where(left if side == 0 else lane >= 64, b, 0.0)
                gram = lax.dot_general(
                    one, jnp.concatenate([one, one], axis=0), (((1,), (1,)), ((), ())),
                    precision=lax.Precision.HIGHEST, preferred_element_type=F32,
                )
                gram = gram + jnp.where(lane == row, SHRINK, 0.0)
                M[n * 2 + side] = jnp.where(left, gram, turned if side == 0 else b)

    place = lax.broadcasted_iota(jnp.int32, (8, 128), 0)
    none = jnp.zeros((8, 128), F32)
    blank = jnp.zeros((16, 128), BF16)
    for kb in range(8):
        heads = [M[p, kb * 8 : kb * 8 + 8, :] for p in range(8)]
        for j in range(8):
            for p in range(8):
                m = heads[p]
                k = kb * 8 + j
                col = jnp.broadcast_to(m[:, k : k + 1], (8, 128))
                scaled = m[j : j + 1] / col[j : j + 1]
                heads[p] = jnp.where(place == j, scaled, m - col * scaled)
        top = slice(kb // 2 * 16, kb // 2 * 16 + 16)
        low = slice(128 + kb // 2 * 16, 144 + kb // 2 * 16)
        for p in range(8):
            if kb % 2 == 0 and kb > 0:
                for lines in (slice(kb // 2 * 16 - 16, kb // 2 * 16), slice(112 + kb // 2 * 16, 128 + kb // 2 * 16)):
                    GA[p, lines, 0:128] = blank
                    GA[p, lines, 128:256] = blank
                    GB[p, lines, :] = blank
            pair = [heads[p], none] if kb % 2 == 0 else [none, heads[p]]
            h1, h2, h3 = split3(jnp.concatenate(pair, axis=0))
            for lines in (top, low):
                GA[p, lines, 0:128] = h1
                GA[p, lines, 128:256] = h2
            GB[p, top, :] = h3
            GB[p, low, :] = h1
        for p in range(8):
            m = M[p]
            m1, m2, m3 = split3(m)
            big = jnp.dot(jnp.concatenate([m1, m2], axis=1), GA[p], preferred_element_type=F32)
            small = jnp.dot(jnp.concatenate([m1, m3], axis=1), GB[p], preferred_element_type=F32)
            M[p] = m - (big[:, 0:128] + (big[:, 128:256] + small))
            M[p, kb * 8 : kb * 8 + 8, :] = heads[p]
    for i in (0, 1):
        for h in (0, 1):
            n = i * 2 + h
            solved = jnp.where(left, pltpu.roll(M[n * 2], 64, axis=1), M[n * 2 + 1])
            b = B[n]
            cols = slice(n * 128, n * 128 + 128)
            new_split = b - SHRINK * solved
            SO[0, :, cols] = new_split
            DO[0, :, cols] = b - new_split
    writes = [pltpu.make_async_copy(SO, split_out, osem.at[0]), pltpu.make_async_copy(DO, dual_out, osem.at[1])]
    for one in writes:
        one.start()
    for one in writes:
        one.wait()
    passed.wait()


def local(tiles, tile_blocks, counts, sino, wts, x0, split, dual):
    n = tile_blocks.reshape(-1)
    tiles_here = n.shape[0]
    src, blk = n // 16, n % 16
    g = blk // 8
    me = lax.axis_index("views")
    across, down = (src - me) % 4, (src // 4 - me // 4) % 4
    place = jnp.where(g == 0, down * 4 + across, across * 4 + down)
    vrow = g * 128 + place * 8 + blk % 8
    order = jnp.arange(tiles_here, dtype=jnp.int32)
    same = (n[:, None] == n[None, :]) & (order[None, :] < order[:, None])
    prev = jnp.max(jnp.where(same, order[None, :] + 1, 0), axis=1)
    rows = jnp.arange(256, dtype=jnp.int32)
    final = jnp.max(jnp.where(rows[:, None] == vrow[None, :], order[None, :] + 1, 0), axis=1)
    idx = jnp.concatenate([vrow, prev, final])
    smem = pl.BlockSpec(memory_space=pltpu.SMEM)
    anywhere = pl.BlockSpec(memory_space=pl.ANY)
    volume, mx, md, step = pl.pallas_call(
        main_kernel,
        out_shape=(
            jax.ShapeDtypeStruct((8, 4096), F32),
            jax.ShapeDtypeStruct((8, 2, 2, 8, 128), F32),
            jax.ShapeDtypeStruct((8, 2, 2, 8, 128), F32),
            jax.ShapeDtypeStruct((8, 8, 128), F32),
        ),
        in_specs=[smem, smem] + [anywhere] * 6,
        out_specs=(anywhere,) * 4,
        scratch_shapes=[
            pltpu.VMEM((2, 4, 24, 256, 256), BF16),
            pltpu.VMEM((NSTAGE, CH, 128, 256), F32),
            *[pltpu.VMEM((256, 8, 128), F32)] * 8,
            pltpu.VMEM((2, 256, 8, 128), F32),
            pltpu.VMEM((3, 2, 2, 3, 24, 8, 128), F32),
            pltpu.VMEM((3, 2, 2, 6, 8, 8, 128), F32),
            pltpu.VMEM((193, 8, 128), F32),
            pltpu.VMEM((2, 2, 8, 8, 128), F32),
            pltpu.VMEM((2, 2, 8, 8, 128), F32),
            pltpu.VMEM((8, 2, 2, 8, 128), F32),
            pltpu.VMEM((3, 8, 2, 2, 8, 128), F32),
            pltpu.VMEM((8, 2, 2, 8, 128), F32),
            pltpu.VMEM((8, 2, 2, 8, 128), F32),
            pltpu.VMEM((8, 8, 128), F32),
            pltpu.VMEM((2, 64, 512), F32),
            pltpu.VMEM((8, 4096), F32),
            pltpu.VMEM((2, 8, 512), F32),
            pltpu.VMEM((8, 4096), F32),
            pltpu.VMEM((4, 8, 128), F32),
            pltpu.VMEM((4, 8, 128), F32),
            pltpu.VMEM((4, 16, 256), BF16),
            pltpu.VMEM((6, 8, 128), F32),
            pltpu.VMEM((7, 8, 128), F32),
            pltpu.VMEM((6, 6, 8, 128), F32),
            pltpu.SemaphoreType.DMA((NSTAGE,)),
            pltpu.SemaphoreType.DMA((5,)),
            pltpu.SemaphoreType.DMA((4,)),
            pltpu.SemaphoreType.DMA((4, 2, 2)),
            pltpu.SemaphoreType.DMA((4, 2, 2, 2)),
            pltpu.SemaphoreType.DMA((3, 2, 2)),
            pltpu.SemaphoreType.DMA((3, 2, 2, 2)),
            pltpu.SemaphoreType.DMA((6, 6)),
            pltpu.SemaphoreType.DMA((6, 6)),
            pltpu.SemaphoreType.DMA((4, 8)),
            pltpu.SemaphoreType.DMA((4, 8)),
        ],
        compiler_params=pltpu.CompilerParams(
            collective_id=0, has_side_effects=True, vmem_limit_bytes=56 * 1024 * 1024
        ),
        name="solve",
    )(idx, counts, tiles, sino, wts, x0, split, dual)
    volume, new_split, new_dual = pl.pallas_call(
        shrink_kernel,
        out_shape=(jax.ShapeDtypeStruct((8, 4096), F32),) + (jax.ShapeDtypeStruct((1, 64, 512), F32),) * 2,
        in_specs=[anywhere] * 5,
        out_specs=(anywhere,) * 3,
        scratch_shapes=[
            pltpu.VMEM((8, 2, 2, 8, 128), F32), pltpu.VMEM((8, 2, 2, 8, 128), F32),
            pltpu.VMEM((8, 8, 128), F32), pltpu.VMEM((1, 64, 512), F32),
            pltpu.VMEM((1, 64, 512), F32), pltpu.VMEM((1, 64, 512), F32),
            pltpu.VMEM((8, 64, 128), F32), pltpu.VMEM((4, 64, 128), F32),
            pltpu.VMEM((8, 256, 256), BF16), pltpu.VMEM((8, 256, 128), BF16),
            pltpu.SemaphoreType.DMA((5,)), pltpu.SemaphoreType.DMA((2,)),
        ],
        compiler_params=pltpu.CompilerParams(vmem_limit_bytes=60 * 1024 * 1024),
        name="shrink",
    )(mx, md, step, dual, volume)
    return volume, new_split, new_dual


def solution(mesh):
    placed = (
        P("views", None, None, None),
        P("views", None),
        P("views"),
        P("energy", "views"),
        P("energy", "views"),
        P("energy", "views"),
        P("views", None, "energy"),
        P("views", None, "energy"),
    )
    return jax.shard_map(
        local,
        mesh=mesh,
        in_specs=placed,
        out_specs=(P("energy", "views"), P("views", None, "energy"), P("views", None, "energy")),
        check_vma=False,
    )
```

```python
import functools

import jax
import jax.numpy as jnp
from jax import lax
from jax.experimental import pallas as pl
from jax.experimental.pallas import tpu as pltpu
from jax.sharding import PartitionSpec as P

PENALTY = 1.0
SHRINK = 16.0
F32 = jnp.float32
BF16 = jnp.bfloat16
NSTAGE = 4
CH = 8


def split2(v):
    hi = v.astype(BF16)
    lo = (v - hi.astype(F32)).astype(BF16)
    return hi, lo


def lane_total(v):
    return jnp.broadcast_to(jnp.sum(v, axis=1, keepdims=True), v.shape)


def main_kernel(
    idx, counts, tiles, sino, wts, x0, split, dual,
    vol_out, mx_out, md_out, step_out,
    W, stage,
    V00, V01, V10, V11, V20, V21, V30, V31,
    F, RB1, RB2, R, X, D, T, TP, MX, MD, MS, SD, XS, RS, VO, Pq, Q, WL, AS, AS2, AR, AL,
    dsem, isem, osem, ag_s, ag_r, rs_s, rs_r, ar_s, ar_r, al_s, al_r, en_s, en_r,
):
    V = ((V00, V01), (V10, V11), (V20, V21), (V30, V31))
    e = lax.axis_index("energy")
    a = lax.axis_index("views")
    y, x = a // 4, a % 4

    def at_views(g, p, s):
        p, s = lax.rem(p + 4, 4), lax.rem(s + 4, 4)
        return {"views": s * 4 + p if g == 0 else p * 4 + s}

    coord = ((x, y), (y, x))

    barrier = pltpu.get_barrier_semaphore()
    for o in range(1, 16):
        pl.semaphore_signal(barrier, inc=1, device_id={"views": lax.rem(a + o, 16)}, device_id_type=pl.DeviceIdType.MESH)
    for o in range(1, 8):
        pl.semaphore_signal(barrier, inc=1, device_id={"energy": lax.rem(e + o, 8)}, device_id_type=pl.DeviceIdType.MESH)

    def tile_copy(c, slot):
        return pltpu.make_async_copy(
            tiles.at[c // 6, pl.ds((c % 6) * CH, CH)], stage.at[slot], dsem.at[slot]
        )

    def read(n):
        to = (SD.at[pl.ds(0, 1)], SD.at[pl.ds(1, 1)], XS, RS.at[0], RS.at[1])[n]
        return pltpu.make_async_copy((split, dual, x0, sino, wts)[n], to, isem.at[n])

    def write(n):
        return pltpu.make_async_copy((MX, MD, MS, VO)[n], (mx_out, md_out, step_out, vol_out)[n], osem.at[n])


    for n in (2, 0, 1, 3, 4):
        read(n).start()
    for c in range(NSTAGE):
        tile_copy(c, c).start()

    def ag(rd, h, g, k):
        p, s = coord[g]
        base, o = g * 128, k % 3 + 1
        src, size, dst, dev = (
            (0, 8, (4 - o) * 8, (p + o, s)),
            (0, 8, (4 - o) * 32, (p, s + o)),
            (8, 24, (4 - o) * 32 + 8, (p, s + o)),
        )[k // 3]
        return pltpu.make_async_remote_copy(
            src_ref=V[rd][h].at[pl.ds(base + src, size)], dst_ref=V[rd][h].at[pl.ds(base + dst, size)],
            send_sem=ag_s.at[rd, h, g], recv_sem=ag_r.at[rd, h, g, min(k // 3, 1)],
            device_id=at_views(g, *dev), device_id_type=pl.DeviceIdType.MESH,
        )

    def ag_bytes(rd, h, g, size, k):
        return pltpu.make_async_remote_copy(
            src_ref=V[rd][h].at[pl.ds(0, size)], dst_ref=V[rd][h].at[pl.ds(0, size)],
            send_sem=ag_s.at[rd, h, g], recv_sem=ag_r.at[rd, h, g, k],
            device_id=at_views(g, coord[g][0] + 1, coord[g][1]), device_id_type=pl.DeviceIdType.MESH,
        )

    def ag_step(rd, h, n):
        if n == 0:
            for k in (0, 2, 1, 3, 5, 4):
                for g in (0, 1):
                    ag(rd, h, g, k).start()
        if n == 1:
            for g in (0, 1):
                ag_bytes(rd, h, g, 24, 0).wait_recv()
                for k in (6, 8, 7):
                    ag(rd, h, g, k).start()
        if n == 2:
            for g in (0, 1):
                ag_bytes(rd, h, g, 96, 1).wait_recv()

    def ag_sent(rd):
        for h in (0, 1):
            for g in (0, 1):
                ag_bytes(rd, h, g, 120, 0).wait_send()

    def rs(rd, h, g, k):
        p, s = coord[g]
        base, o = g * 128, k % 3 + 1
        src, size, dev = (
            (o * 32 + 8, 24, (p, s + o)),
            (o * 32, 8, (p, s + o)),
            (o * 8, 8, (p + o, s)),
        )[k // 3]
        land = RB1.at[rd, h, g, k] if k < 3 else RB2.at[rd, h, g, k - 3]
        return pltpu.make_async_remote_copy(
            src_ref=F.at[h, pl.ds(base + src, size)], dst_ref=land,
            send_sem=rs_s.at[rd, h, g], recv_sem=rs_r.at[rd, h, g, min(k // 3, 1)],
            device_id=at_views(g, *dev), device_id_type=pl.DeviceIdType.MESH,
        )

    def rs_bytes(rd, h, g, size, k):
        return pltpu.make_async_remote_copy(
            src_ref=F.at[h, pl.ds(0, size)], dst_ref=F.at[h, pl.ds(0, size)],
            send_sem=rs_s.at[rd, h, g], recv_sem=rs_r.at[rd, h, g, k],
            device_id=at_views(g, coord[g][0] + 1, coord[g][1]), device_id_type=pl.DeviceIdType.MESH,
        )

    def rs_step(rd, h, n):
        if n == 0:
            for k in (0, 2, 1, 3, 5, 4):
                for g in (0, 1):
                    rs(rd, h, g, k).start()
        if n == 1:
            for g in (0, 1):
                rs_bytes(rd, h, g, 72, 0).wait_recv()
                line = pl.ds(g * 128 + 8, 24)
                F[h, line] = F[h, line] + RB1[rd, h, g, 0] + RB1[rd, h, g, 1] + RB1[rd, h, g, 2]
                for k in (6, 8, 7):
                    rs(rd, h, g, k).start()
        if n == 2:
            for g in (0, 1):
                rs_bytes(rd, h, g, 48, 1).wait_recv()

    def rs_total(rd, h, g):
        total = F[h, own_rows(g)]
        for k in range(6):
            total = total + RB2[rd, h, g, k]
        return total

    def rs_sent(rd):
        for h in (0, 1):
            for g in (0, 1):
                rs_bytes(rd, h, g, 120, 0).wait_send()

    def ar(n, k):
        src = AS if k < 3 else AS2
        o = k % 3 + 1
        dev = at_views(0, x + o, y) if k < 3 else at_views(0, x, y + o)
        return pltpu.make_async_remote_copy(
            src_ref=src.at[n], dst_ref=AR.at[n, k],
            send_sem=ar_s.at[n], recv_sem=ar_r.at[n, k // 3],
            device_id=dev, device_id_type=pl.DeviceIdType.MESH,
        )

    def ar_bytes(n, size, k):
        return pltpu.make_async_remote_copy(
            src_ref=AR.at[n, pl.ds(0, size)], dst_ref=AR.at[n, pl.ds(0, size)],
            send_sem=ar_s.at[n], recv_sem=ar_r.at[n, k],
            device_id=at_views(0, x + 1, y), device_id_type=pl.DeviceIdType.MESH,
        )

    def ar_start(n, value):
        AS[n] = value
        for k in range(3):
            ar(n, k).start()

    def ar_mid(n):
        ar_bytes(n, 3, 0).wait_recv()
        AS2[n] = AS[n] + AR[n, 0] + AR[n, 1] + AR[n, 2]
        for k in range(3, 6):
            ar(n, k).start()

    def ar_end(n):
        ar_bytes(n, 3, 1).wait_recv()
        total = AS2[n] + AR[n, 3] + AR[n, 4] + AR[n, 5]
        ar_bytes(n, 6, 0).wait_send()
        return lane_total(total)

    def last_sum(o):
        return pltpu.make_async_remote_copy(
            src_ref=AS.at[5], dst_ref=AL.at[o - 1], send_sem=al_s, recv_sem=al_r,
            device_id={"views": lax.rem(a + o, 16)}, device_id_type=pl.DeviceIdType.MESH,
        )

    def last_bytes():
        ref = AL.at[pl.ds(0, 15)]
        return pltpu.make_async_remote_copy(
            src_ref=ref, dst_ref=ref, send_sem=al_s, recv_sem=al_r,
            device_id={"views": lax.rem(a + 1, 16)}, device_id_type=pl.DeviceIdType.MESH,
        )

    def en(n, o):
        to = lax.rem(e + o, 8)
        src = TP.at[n, to] if n < 3 else AS2.at[6]
        return pltpu.make_async_remote_copy(
            src_ref=src, dst_ref=(T, MX, MD, MS)[n].at[e],
            send_sem=en_s.at[n], recv_sem=en_r.at[n],
            device_id={"energy": to}, device_id_type=pl.DeviceIdType.MESH,
        )

    def en_bytes(n):
        ref = (T, MX, MD, MS)[n].at[pl.ds(0, 7)]
        return pltpu.make_async_remote_copy(
            src_ref=ref, dst_ref=ref, send_sem=en_s.at[n], recv_sem=en_r.at[n],
            device_id={"energy": lax.rem(e + 1, 8)}, device_id_type=pl.DeviceIdType.MESH,
        )

    def en_volume(n, what):
        for to in range(8):
            for i in (0, 1):
                blk = 2 * to + i
                for h in (0, 1):
                    TP[n, to, i, h] = what[h, blk // 8, blk % 8]
        for o in range(1, 8):
            en(n, o).start()
        (T, MX, MD)[n][e] = TP[n, e]

    def own_rows(g):
        return pl.ds(g * 128, 8)

    read(2).wait()
    for h in (0, 1):
        for blk in range(16):
            piece = XS[:, blk * 256 + h * 128 : blk * 256 + h * 128 + 128]
            X[h, blk // 8, blk % 8] = piece
        for g in (0, 1):
            V[0][h][own_rows(g)] = X[h, g]
    pl.semaphore_wait(barrier, 22)
    for h in (0, 1):
        ag_step(0, h, 0)

    for n in (0, 1, 3, 4):
        read(n).wait()
    for to in range(8):
        for i in (0, 1):
            for h in (0, 1):
                cols = slice(i * 256 + h * 128, i * 256 + h * 128 + 128)
                rows = slice(to * 8, to * 8 + 8)
                TP[0, to, i, h] = SD[0, rows, cols] - SD[1, rows, cols]
    T[e] = TP[0, e]
    for o in range(1, 8):
        en(0, o).start()

    R[0] = jnp.zeros((8, 128), F32)

    def convert(c, carry):
        slot = lax.rem(c, NSTAGE)
        tile_copy(c, slot).wait()
        b = c // 6
        for u in range(CH // 2):
            jp = (c % 6) * (CH // 2) + u
            for h in (0, 1):
                for t in (0, 1):
                    part = stage[slot, 2 * u + t, :, h * 128 : h * 128 + 128]
                    here = slice(t * 128, t * 128 + 128)
                    if h == 0:
                        W[h, b, jp, 0:128, here], W[h, b, jp, 128:256, here] = split2(part)
                    else:
                        W[h, b, jp, here, 0:128], W[h, b, jp, here, 128:256] = split2(part.T)

        @pl.when(c + NSTAGE < 24)
        def _():
            tile_copy(c + NSTAGE, slot).start()

        return carry

    def fwd(rd, h, lo_b, hi_b):
        def body(b, carry):
            acc = jnp.zeros((16, 256), F32)
            for jp in range(24):
                i = b * 48 + 2 * jp
                v0 = V[rd][h][idx[i]]
                v1 = V[rd][h][idx[i + 1]]
                hi, lo = split2(jnp.concatenate([v0, v1], axis=1))
                acc = acc + lax.dot_general(
                    jnp.concatenate([hi, lo], axis=0), W[h, b, jp],
                    (((1,), (1 - h,)), ((), ())), preferred_element_type=F32,
                )
            both = acc[0:8] + acc[8:16]
            part = both[:, 0:128] + both[:, 128:256]
            if h == 0:
                Pq[b] = part
            else:
                Pq[b] = Pq[b] + part
            return carry

        lax.fori_loop(lo_b, hi_b, body, 0)

    def bwd(h, lo_b, hi_b):
        def body(b, carry):
            lhs = WL[b]
            for jp in range(24):
                i = b * 48 + 2 * jp
                out = lax.dot_general(
                    lhs, W[h, b, jp], (((1,), (h,)), ((), ())), preferred_element_type=F32
                )
                both = out[0:8] + out[8:16]
                R[i + 1] = both[:, 0:128] + R[idx[192 + i]]
                R[i + 2] = both[:, 128:256] + R[idx[193 + i]]
            return carry

        lax.fori_loop(lo_b, hi_b, body, 0)

    def scatter(h):
        def body(n, carry):
            for j in range(8):
                F[h, n * 8 + j] = R[idx[384 + n * 8 + j]]
            return carry

        lax.fori_loop(0, 32, body, 0)

    lane = lax.broadcasted_iota(jnp.int32, (8, 128), 1)

    def scale(b):
        return jnp.where(lane < counts[b], RS[1, :, b * 128 : b * 128 + 128], 0.0)

    def squares(v):
        return jnp.sum(v * v, axis=0)

    lax.fori_loop(0, 10, convert, 0)
    ag_step(0, 0, 1)
    ag_step(0, 1, 1)
    lax.fori_loop(10, 24, convert, 0)

    rr = None
    for rd in range(4):
        last = rd == 3
        ag_step(rd, 0, 2)
        fwd(rd, 0, 0, 2)
        if rd > 0:
            ar_mid(2 * rd - 2)
        fwd(rd, 0, 2, 4)
        ag_step(rd, 1, 2)
        fwd(rd, 1, 0, 4)
        if rd == 0:
            for b in range(4):
                w = scale(b) * (RS[0, :, b * 128 : b * 128 + 128] - Pq[b])
                hi, lo = split2(w)
                WL[b] = jnp.concatenate(
                    [jnp.concatenate([hi, hi], axis=1), jnp.concatenate([lo, lo], axis=1)], axis=0
                )
        else:
            rr_new = ar_end(2 * rd - 2)
            curv = jnp.zeros((8, 128), F32)
            if rd > 1:
                beta = rr_new / rr
            rr = rr_new
            for h in (0, 1):
                for g in (0, 1):
                    r_own = V[rd][h][own_rows(g)]
                    d_own = r_own if rd == 1 else r_own + beta * D[h, g]
                    D[h, g] = d_own
                    curv = curv + PENALTY * squares(d_own)
            for b in range(4):
                q = Pq[b] if rd == 1 else Pq[b] + beta * Q[b]
                Q[b] = q
                w = scale(b) * q
                curv = curv + w * q
                if not last:
                    hi, lo = split2(w)
                    WL[b] = jnp.concatenate(
                        [jnp.concatenate([hi, hi], axis=1), jnp.concatenate([lo, lo], axis=1)], axis=0
                    )
            if last:
                AS[5] = curv
                for o in (10, 6, 9, 11, 5, 7, 2, 8, 14, 3, 13, 1, 4, 12, 15):
                    last_sum(o).start()
            else:
                ar_start(2 * rd - 1, curv)
        if not last:
            bwd(0, 0, 4)
            scatter(0)
            rs_step(rd, 0, 0)
            bwd(1, 0, 2)
            if rd > 0:
                ar_mid(2 * rd - 1)
            bwd(1, 2, 4)
            scatter(1)
            rs_step(rd, 1, 0)
            ag_sent(rd)
            rs_step(rd, 0, 1)
            rs_step(rd, 1, 1)
            if rd > 0:
                alpha = rr / ar_end(2 * rd - 1)
            else:
                en_bytes(0).wait_recv()
            norm = jnp.zeros((8, 128), F32)
            for h in (0, 1):
                for g in (0, 1):
                    rs_bytes(rd, h, g, 48, 1).wait_recv()
                    summed = rs_total(rd, h, g)
                    if rd == 0:
                        anchor = T[g * 4 : g * 4 + 4, :, h].reshape(8, 8, 128)
                        r_own = summed + PENALTY * (anchor - X[h, g])
                    else:
                        d_own = D[h, g]
                        r_own = V[rd][h][own_rows(g)] - alpha * (summed + PENALTY * d_own)
                        X[h, g] = X[h, g] + alpha * d_own
                    V[rd + 1][h][own_rows(g)] = r_own
                    norm = norm + squares(r_own)
                    for k in (0, 2, 1, 3, 5, 4):
                        ag(rd + 1, h, g, k).start()
            ar_start(2 * rd, norm)
            ag_step(rd + 1, 0, 1)
            ag_step(rd + 1, 1, 1)
            rs_sent(rd)
            if rd == 2:
                en_volume(1, X)
        else:
            en_volume(2, D)
            ag_sent(rd)
            last_bytes().wait_recv()
            total = AS[5]
            for o in range(15):
                total = total + AL[o]
            alpha = rr / lane_total(total)
            AS2[6] = alpha
            MS[e] = alpha
            for o in range(1, 8):
                en(3, o).start()
            for h in (0, 1):
                for blk in range(16):
                    cols = slice(blk * 256 + h * 128, blk * 256 + h * 128 + 128)
                    VO[:, cols] = X[h, blk // 8, blk % 8] + alpha * D[h, blk // 8, blk % 8]
    write(3).start()
    for n in (1, 2, 3):
        en_bytes(n).wait_recv()
        write(n - 1).start()
    for n in range(4):
        en_bytes(n).wait_send()
    last_bytes().wait_send()
    for n in range(4):
        write(n).wait()


def split3(v):
    a = v.astype(BF16)
    rest = v - a.astype(F32)
    b = rest.astype(BF16)
    return a, b, (rest - b.astype(F32)).astype(BF16)


def shrink_kernel(
    mx_in, md_in, step_in, dual_in, vol, vol_out, split_out, dual_out,
    mx, md, step, dual, SO, DO, M, B, GA, GB, isem, osem,
):
    passed = pltpu.make_async_copy(vol, vol_out, isem.at[4])
    passed.start()
    reads = [
        pltpu.make_async_copy(a, b, isem.at[n])
        for n, (a, b) in enumerate(((mx_in, mx), (md_in, md), (step_in, step), (dual_in, dual)))
    ]
    for one in reads:
        one.start()
    GA[...] = jnp.zeros_like(GA)
    GB[...] = jnp.zeros_like(GB)
    for one in reads:
        one.wait()
    steps = step[...].reshape(64, 128)
    lane = lax.broadcasted_iota(jnp.int32, (64, 128), 1)
    row = lax.broadcasted_iota(jnp.int32, (64, 128), 0)
    left = lane < 64
    for i in (0, 1):
        for h in (0, 1):
            n = i * 2 + h
            volume = mx[:, i, h].reshape(64, 128) + steps * md[:, i, h].reshape(64, 128)
            b = volume + dual[0, :, n * 128 : n * 128 + 128]
            B[n] = b
            turned = pltpu.roll(b, 64, axis=1)
            for side in (0, 1):
                one = jnp.where(left if side == 0 else lane >= 64, b, 0.0)
                gram = lax.dot_general(
                    one, jnp.concatenate([one, one], axis=0), (((1,), (1,)), ((), ())),
                    precision=lax.Precision.HIGHEST, preferred_element_type=F32,
                )
                gram = gram + jnp.where(lane == row, SHRINK, 0.0)
                M[n * 2 + side] = jnp.where(left, gram, turned if side == 0 else b)

    place = lax.broadcasted_iota(jnp.int32, (8, 128), 0)
    none = jnp.zeros((8, 128), F32)
    blank = jnp.zeros((16, 128), BF16)
    for kb in range(8):
        heads = [M[p, kb * 8 : kb * 8 + 8, :] for p in range(8)]
        for j in range(8):
            for p in range(8):
                m = heads[p]
                k = kb * 8 + j
                col = jnp.broadcast_to(m[:, k : k + 1], (8, 128))
                scaled = m[j : j + 1] / col[j : j + 1]
                heads[p] = jnp.where(place == j, scaled, m - col * scaled)
        top = slice(kb // 2 * 16, kb // 2 * 16 + 16)
        low = slice(128 + kb // 2 * 16, 144 + kb // 2 * 16)
        for p in range(8):
            if kb % 2 == 0 and kb > 0:
                for lines in (slice(kb // 2 * 16 - 16, kb // 2 * 16), slice(112 + kb // 2 * 16, 128 + kb // 2 * 16)):
                    GA[p, lines, 0:128] = blank
                    GA[p, lines, 128:256] = blank
                    GB[p, lines, :] = blank
            pair = [heads[p], none] if kb % 2 == 0 else [none, heads[p]]
            h1, h2, h3 = split3(jnp.concatenate(pair, axis=0))
            for lines in (top, low):
                GA[p, lines, 0:128] = h1
                GA[p, lines, 128:256] = h2
            GB[p, top, :] = h3
            GB[p, low, :] = h1
        for p in range(8):
            m = M[p]
            m1, m2, m3 = split3(m)
            big = jnp.dot(jnp.concatenate([m1, m2], axis=1), GA[p], preferred_element_type=F32)
            small = jnp.dot(jnp.concatenate([m1, m3], axis=1), GB[p], preferred_element_type=F32)
            M[p] = m - (big[:, 0:128] + (big[:, 128:256] + small))
            M[p, kb * 8 : kb * 8 + 8, :] = heads[p]
    for i in (0, 1):
        for h in (0, 1):
            n = i * 2 + h
            solved = jnp.where(left, pltpu.roll(M[n * 2], 64, axis=1), M[n * 2 + 1])
            b = B[n]
            cols = slice(n * 128, n * 128 + 128)
            new_split = b - SHRINK * solved
            SO[0, :, cols] = new_split
            DO[0, :, cols] = b - new_split
    writes = [pltpu.make_async_copy(SO, split_out, osem.at[0]), pltpu.make_async_copy(DO, dual_out, osem.at[1])]
    for one in writes:
        one.start()
    for one in writes:
        one.wait()
    passed.wait()


def local(tiles, tile_blocks, counts, sino, wts, x0, split, dual):
    n = tile_blocks.reshape(-1)
    tiles_here = n.shape[0]
    src, blk = n // 16, n % 16
    g = blk // 8
    me = lax.axis_index("views")
    across, down = (src - me) % 4, (src // 4 - me // 4) % 4
    place = jnp.where(g == 0, down * 4 + across, across * 4 + down)
    vrow = g * 128 + place * 8 + blk % 8
    order = jnp.arange(tiles_here, dtype=jnp.int32)
    same = (n[:, None] == n[None, :]) & (order[None, :] < order[:, None])
    prev = jnp.max(jnp.where(same, order[None, :] + 1, 0), axis=1)
    rows = jnp.arange(256, dtype=jnp.int32)
    final = jnp.max(jnp.where(rows[:, None] == vrow[None, :], order[None, :] + 1, 0), axis=1)
    idx = jnp.concatenate([vrow, prev, final])
    smem = pl.BlockSpec(memory_space=pltpu.SMEM)
    anywhere = pl.BlockSpec(memory_space=pl.ANY)
    volume, mx, md, step = pl.pallas_call(
        main_kernel,
        out_shape=(
            jax.ShapeDtypeStruct((8, 4096), F32),
            jax.ShapeDtypeStruct((8, 2, 2, 8, 128), F32),
            jax.ShapeDtypeStruct((8, 2, 2, 8, 128), F32),
            jax.ShapeDtypeStruct((8, 8, 128), F32),
        ),
        in_specs=[smem, smem] + [anywhere] * 6,
        out_specs=(anywhere,) * 4,
        scratch_shapes=[
            pltpu.VMEM((2, 4, 24, 256, 256), BF16),
            pltpu.VMEM((NSTAGE, CH, 128, 256), F32),
            *[pltpu.VMEM((256, 8, 128), F32)] * 8,
            pltpu.VMEM((2, 256, 8, 128), F32),
            pltpu.VMEM((3, 2, 2, 3, 24, 8, 128), F32),
            pltpu.VMEM((3, 2, 2, 6, 8, 8, 128), F32),
            pltpu.VMEM((193, 8, 128), F32),
            pltpu.VMEM((2, 2, 8, 8, 128), F32),
            pltpu.VMEM((2, 2, 8, 8, 128), F32),
            pltpu.VMEM((8, 2, 2, 8, 128), F32),
            pltpu.VMEM((3, 8, 2, 2, 8, 128), F32),
            pltpu.VMEM((8, 2, 2, 8, 128), F32),
            pltpu.VMEM((8, 2, 2, 8, 128), F32),
            pltpu.VMEM((8, 8, 128), F32),
            pltpu.VMEM((2, 64, 512), F32),
            pltpu.VMEM((8, 4096), F32),
            pltpu.VMEM((2, 8, 512), F32),
            pltpu.VMEM((8, 4096), F32),
            pltpu.VMEM((4, 8, 128), F32),
            pltpu.VMEM((4, 8, 128), F32),
            pltpu.VMEM((4, 16, 256), BF16),
            pltpu.VMEM((6, 8, 128), F32),
            pltpu.VMEM((7, 8, 128), F32),
            pltpu.VMEM((6, 6, 8, 128), F32),
            pltpu.VMEM((15, 8, 128), F32),
            pltpu.SemaphoreType.DMA((NSTAGE,)),
            pltpu.SemaphoreType.DMA((5,)),
            pltpu.SemaphoreType.DMA((4,)),
            pltpu.SemaphoreType.DMA((4, 2, 2)),
            pltpu.SemaphoreType.DMA((4, 2, 2, 2)),
            pltpu.SemaphoreType.DMA((3, 2, 2)),
            pltpu.SemaphoreType.DMA((3, 2, 2, 2)),
            pltpu.SemaphoreType.DMA((6,)),
            pltpu.SemaphoreType.DMA((6, 2)),
            pltpu.SemaphoreType.DMA,
            pltpu.SemaphoreType.DMA,
            pltpu.SemaphoreType.DMA((4,)),
            pltpu.SemaphoreType.DMA((4,)),
        ],
        compiler_params=pltpu.CompilerParams(
            collective_id=0, has_side_effects=True, vmem_limit_bytes=56 * 1024 * 1024
        ),
        name="solve",
    )(idx, counts, tiles, sino, wts, x0, split, dual)
    volume, new_split, new_dual = pl.pallas_call(
        shrink_kernel,
        out_shape=(jax.ShapeDtypeStruct((8, 4096), F32),) + (jax.ShapeDtypeStruct((1, 64, 512), F32),) * 2,
        in_specs=[anywhere] * 5,
        out_specs=(anywhere,) * 3,
        scratch_shapes=[
            pltpu.VMEM((8, 2, 2, 8, 128), F32), pltpu.VMEM((8, 2, 2, 8, 128), F32),
            pltpu.VMEM((8, 8, 128), F32), pltpu.VMEM((1, 64, 512), F32),
            pltpu.VMEM((1, 64, 512), F32), pltpu.VMEM((1, 64, 512), F32),
            pltpu.VMEM((8, 64, 128), F32), pltpu.VMEM((4, 64, 128), F32),
            pltpu.VMEM((8, 256, 256), BF16), pltpu.VMEM((8, 256, 128), BF16),
            pltpu.SemaphoreType.DMA((5,)), pltpu.SemaphoreType.DMA((2,)),
        ],
        compiler_params=pltpu.CompilerParams(vmem_limit_bytes=60 * 1024 * 1024),
        name="shrink",
    )(mx, md, step, dual, volume)
    return volume, new_split, new_dual


def solution(mesh):
    placed = (
        P("views", None, None, None),
        P("views", None),
        P("views"),
        P("energy", "views"),
        P("energy", "views"),
        P("energy", "views"),
        P("views", None, "energy"),
        P("views", None, "energy"),
    )
    return jax.shard_map(
        local,
        mesh=mesh,
        in_specs=placed,
        out_specs=(P("energy", "views"), P("views", None, "energy"), P("views", None, "energy")),
        check_vma=False,
    )
```
